256 devices in a mesh: rep: 4 (over z_lo), fsdp: 64 (over y, x, z_hi, core).
Axes of the slice: x: 4, y: 4, z: 8 (z_hi: 2, z_lo: 4; z = z_hi * 4 + z_lo), core: 2. Of those that a mesh axis runs over, the one named last changes fastest.
Arguments:
- step_index: int32 [1], replicated, may hold values from 0 to 63
- tokens: bfloat16 [4, 32768, 2304], P('rep', 'fsdp'), may hold values from -16 to 16
- queries: bfloat16 [4, 32768, 2048], P('rep', 'fsdp'), may hold values from -128 to 128
- cotangent: bfloat16 [4, 32768, 2048], P('rep', 'fsdp'), may hold values from -6 to 6
- params: float32 [4, 2304, 2048], P('rep', 'fsdp'), may hold values from -6 to 6
- momentum: float32 [4, 2304, 2048], P('rep', 'fsdp'), may hold values from -6 to 6
Outputs:
- new_params: float32 [4, 2304, 2048], P('rep', 'fsdp')
- new_moments: float32 [4, 2304, 2048], P('rep', 'fsdp')
The draws below stay inside these ranges and needn't reach their ends.
All inputs are finite; a program needn't handle non-finite values.
Results may differ from the reference program's by a relative error of at most 0.006.
The reference program's roundings to bfloat16 on the way count: a program that leaves them out, or rounds other values in their place, can miss the bound.
Values may be sent and summed in bfloat16 or wider, within the bound.
A program may use at most 128 MiB of HBM per device.

```python
import jax
import jax.numpy as jnp
from jax import lax

D = 2304
QH = 16
KVH = 8
HEAD = 128
LENGTH = 256
QW = 2048
KVW = 2048
TOKENS = 32768
REPLICAS = 4
N_REP = 4


def draw_queries(key, part):
    key = jax.random.fold_in(key, 7)
    order_key, value_key = jax.random.split(key)
    order = jax.random.permutation(order_key, QH).astype(jnp.float32)
    exponent = order / max(QH - 1, 1)
    head_scale = 32.0 ** exponent
    base = jnp.clip(jax.random.normal(value_key, (REPLICAS, TOKENS, QH, HEAD), jnp.float32), -4.0, 4.0)
    values = base * head_scale[None, None, :, None]
    return values.reshape(REPLICAS, TOKENS, QH * HEAD).astype(jnp.bfloat16)


def strengthened(array, stream_key, source, target, parts, factor):
    owner, partner = [(jnp.arange(array.shape[position]) // (array.shape[position] // parts)).reshape([-1 if axis == position else 1 for axis in range(array.ndim)]) for position in (source, target)]
    chosen = jax.random.permutation(stream_key, parts)[partner]
    strong = (owner == chosen) | (owner == (partner + parts // 2) % parts)
    return jnp.where(strong, factor * array, array)


def level_of(key, shape, cuts, low, top_value):
    def one(axis_at, shards_of):
        steps = jax.random.uniform(jax.random.fold_in(jax.random.fold_in(key, 6), axis_at), (shards_of,), jnp.float32, low / len(cuts), top_value / len(cuts))
        return jnp.repeat(jnp.exp(steps), shape[axis_at] // shards_of).reshape((-1,) + (1,) * (len(shape) - axis_at - 1))

    gain = one(*cuts[0])
    for cut in cuts[1:]:
        gain = gain * one(*cut)
    return gain


def normal_values(rng, dims, scale, limit, shards=(), held_as=jnp.bfloat16):
    array = jax.random.normal(rng, dims, jnp.float32) * scale
    if len(shards) > 0:
        array = level_of(rng, dims, shards, -0.22, 0.18) * array
    return jnp.clip(array, min=-limit, max=limit).astype(held_as)


def gaussian_with(rng, dims, width, most, cuts, heavy, held_as=jnp.bfloat16):
    values = width * jax.random.normal(rng, dims, jnp.float32)
    if cuts:
        values = values * level_of(rng, dims, cuts, -0.22, 0.18)
    return jnp.clip(strengthened(values, jax.random.fold_in(rng, 3), *heavy), -most, most).astype(held_as)


def setup_inputs(seed: int = 0) -> dict:
    splits = jax.random.split(jax.random.key(seed), 7)
    step_index = jax.random.randint(splits[0], (1,), 0, 64).astype(jnp.int32)
    tokens = gaussian_with(splits[1], (REPLICAS, TOKENS, D), 1.0, 16.0, ((0, 4), (1, 64)), (1, 2, 64, 4.0))
    queries = draw_queries(jax.random.fold_in(splits[6], 71), 0)
    cotangent = normal_values(splits[3], (REPLICAS, TOKENS, QW), 0.8, 6.0, ((0, 4), (1, 64)))
    params = normal_values(splits[4], (REPLICAS, D, KVW), 1.0, 6.0, ((0, 4), (1, 64)), jnp.float32)
    momentum = normal_values(splits[5], (REPLICAS, D, KVW), 0.5, 6.0, ((0, 4), (1, 64)), jnp.float32)
    return dict(step_index=step_index, tokens=tokens, queries=queries, cotangent=cotangent, params=params, momentum=momentum)


SOFT_CAP = 50.0
SCORE_SCALE = 144.0 ** -0.5
ROPE_THETA = 10000.0
LEARN_RATE = 0.1
WARM_SPAN = 64.0
MOMENTUM_DECAY = 0.9


def rope_tables():
    half_head = HEAD // 2
    inverse = ROPE_THETA ** (-jnp.arange(half_head, dtype=jnp.float32) / half_head)
    angles = jnp.arange(LENGTH, dtype=jnp.float32)[:, None] * inverse[None, :]
    return jnp.cos(angles), jnp.sin(angles)


def sequence_grads(block, cosine, sine_table):
    query_rows, key_rows, value_rows, upstream = block
    groups = QH // KVH
    half_head = HEAD // 2
    query_five = query_rows.astype(jnp.float32).reshape(LENGTH, KVH, groups, HEAD)
    upstream_five = upstream.astype(jnp.float32).reshape(LENGTH, KVH, groups, HEAD)
    key_heads = key_rows.astype(jnp.float32).reshape(LENGTH, KVH, HEAD)
    value_heads = value_rows.astype(jnp.float32).reshape(LENGTH, KVH, HEAD)
    cos_rows = cosine[:, None, :]
    sin_rows = sine_table[:, None, :]
    lower = key_heads[..., :half_head]
    upper = key_heads[..., half_head:]
    rotated_low = lax.optimization_barrier(jnp.concatenate([lower * cos_rows - upper * sin_rows, upper * cos_rows + lower * sin_rows], axis=-1).astype(jnp.bfloat16))
    rotated = rotated_low.astype(jnp.float32)
    scores = jnp.einsum("qngd,knd->ngqk", query_five, rotated, precision=lax.Precision.HIGHEST) * SCORE_SCALE
    bent = jnp.tanh(scores / SOFT_CAP)
    causal = jnp.arange(LENGTH)[:, None] >= jnp.arange(LENGTH)[None, :]
    weights = jnp.where(causal, jnp.exp(SOFT_CAP * bent), 0.0)
    shares = weights / jnp.sum(weights, axis=-1, keepdims=True)
    shares_low = lax.optimization_barrier(shares.astype(jnp.bfloat16)).astype(jnp.float32)
    value_grad = jnp.einsum("ngqk,qngd->knd", shares_low, upstream_five, precision=lax.Precision.HIGHEST)
    share_grad = jnp.einsum("qngd,knd->ngqk", upstream_five, value_heads, precision=lax.Precision.HIGHEST)
    score_grad = shares * (share_grad - jnp.sum(shares * share_grad, axis=-1, keepdims=True)) * (1.0 - bent * bent) * SCORE_SCALE
    score_low = lax.optimization_barrier(score_grad.astype(jnp.bfloat16)).astype(jnp.float32)
    rotated_grad = jnp.einsum("ngqk,qngd->knd", score_low, query_five, precision=lax.Precision.HIGHEST)
    lower_grad = rotated_grad[..., :half_head]
    upper_grad = rotated_grad[..., half_head:]
    key_grad = jnp.concatenate([lower_grad * cos_rows + upper_grad * sin_rows, upper_grad * cos_rows - lower_grad * sin_rows], axis=-1)
    return key_grad.reshape(LENGTH, KVH * HEAD), value_grad.reshape(LENGTH, KVH * HEAD)


def reference(step_index, tokens, queries, cotangent, params, momentum):
    cosine, sine_table = rope_tables()
    scale_in = D ** -0.5
    key_width = KVH * HEAD
    sequences = TOKENS // LENGTH
    learn_now = LEARN_RATE * (step_index[0].astype(jnp.float32) + 1.0) / WARM_SPAN

    def per_block(block):
        return sequence_grads(block, cosine, sine_table)

    moved_params = []
    moved_moments = []
    for replica in range(N_REP):
        tok_rows = tokens[replica]
        weights_low = params[replica].astype(jnp.bfloat16)
        joined = (jnp.dot(tok_rows, weights_low, preferred_element_type=jnp.float32) * scale_in).astype(jnp.bfloat16)
        blocks = (queries[replica].reshape(sequences, LENGTH, QH * HEAD),
                  joined[:, :key_width].reshape(sequences, LENGTH, key_width),
                  joined[:, key_width:].reshape(sequences, LENGTH, key_width),
                  cotangent[replica].reshape(sequences, LENGTH, QH * HEAD))
        key_grad, value_grad = lax.map(per_block, blocks)
        both_grads = (jnp.concatenate([key_grad.reshape(TOKENS, key_width), value_grad.reshape(TOKENS, key_width)], axis=1) * scale_in).astype(jnp.bfloat16)
        gradient = jnp.dot(tok_rows.T, both_grads, preferred_element_type=jnp.float32)
        moment = MOMENTUM_DECAY * momentum[replica] + gradient
        moved_moments.append(moment)
        moved_params.append(params[replica] - learn_now * moment)
    stepped_params = jnp.stack(moved_params)
    stepped_moments = jnp.stack(moved_moments)
    levels = N_REP.bit_length() - 1
    distance = jnp.left_shift(jnp.ones((), jnp.int32), step_index[0] % levels)
    sources = (jnp.arange(N_REP, dtype=jnp.int32) - distance) % N_REP
    new_params = 0.5 * (stepped_params + stepped_params[sources])
    new_moments = 0.5 * (stepped_moments + stepped_moments[sources])
    return new_params, new_moments
```

```python
import functools

import jax
import jax.numpy as jnp
import numpy as np
from jax import lax
from jax.experimental import pallas as pl
from jax.experimental.pallas import tpu as pltpu
from jax.sharding import PartitionSpec as P

MESH = pl.DeviceIdType.MESH
F32 = jnp.float32
BF16 = jnp.bfloat16

HEAD = 128
LENGTH = 256
SOFT_CAP = 50.0
SCORE_SCALE = 144.0 ** (-0.5)
ROPE_THETA = 10000.0
LEARN_RATE = 0.1
WARM_SPAN = 64.0
MOMENTUM_DECAY = 0.9

D = 2304
TOK = 512
CH = 4
ROWS = 144
OWN = 36
WIDE = 2048

M_QUAD = 0
M_AG = 3
M_RS = 19
M_Z = 43
M_FIX = 44
M_GOS = 45
M_ALL = 49


def rope_tables():
    half = HEAD // 2
    inverse = np.float32(ROPE_THETA) ** (-np.arange(half, dtype=np.float32) / np.float32(half))
    angles = np.arange(LENGTH, dtype=np.float32)[:, None] * inverse[None, :].astype(np.float32)
    cos, sin = np.cos(angles), np.sin(angles)
    cos_full = np.concatenate([cos, cos], axis=1).astype(np.float32)
    sin_signed = np.concatenate([-sin, sin], axis=1).astype(np.float32)
    return cos_full, sin_signed


def m16(value, by=16):
    return pl.multiple_of(value, by)


SCRATCH = dict(
    tok=((2 * TOK, D), BF16),
    tok_t=((D, 2 * TOK), BF16),
    q=((2 * TOK, 1024), BF16),
    cot=((2 * TOK, 1024), BF16),
    p=((OWN, WIDE), F32),
    m=((OWN, WIDE), F32),
    peer=((2, 2, OWN, WIDE), F32),
    piece=((CH, 2, 48, 256), BF16),
    pin=((CH, 4, 48, 256), BF16),
    w=((CH, 4, 576, 256), BF16),
    grads=((2 * TOK, 256), BF16),
    f=((CH, 4, 576, 256), F32),
    g=((CH, 4, 576, 256), BF16),
    h=((CH, 2, 4, ROWS, 128), F32),
    hb=((CH, 2, 4, ROWS, 128), BF16),
    e=((CH, ROWS, 256), F32),
    zs=((CH, 80, 256), BF16),
    zr=((CH, 80, 256), BF16),
    fs=((CH, 40, 256), F32),
    gx=((CH, 2, 40, 256), F32),
    gb=((CH, 2, 48, 256), BF16),
    gp=((2, CH, 2, 48, 256), BF16),
)
PARTS = ("al", "bl", "cl", "ar", "br", "cr", "tr", "tl")
P_PARTS = ("al", "cl", "br", "tr")
for _name in PARTS:
    SCRATCH["x0" + _name] = ((CH, 2, ROWS, 128), BF16)
    SCRATCH["x1" + _name] = ((CH, 288, 128), BF16)
    for _half in (0, 1):
        SCRATCH["y%d%s" % (_half, _name)] = ((CH, 80 if _name in P_PARTS else 64, 128), BF16)
NAMES = tuple(SCRATCH)


def kernel(step_ref, tok_h, q_h, cot_h, p_h, m_h, cos_ref, sin_ref, outp_ref, outm_ref, *scratch):
    b = dict(zip(NAMES, scratch))
    ssem, rsem, gssem, grsem, lsem = scratch[len(NAMES):]
    rep = lax.axis_index("rep")
    f = lax.axis_index("fsdp")
    core = lax.rem(f, 2)
    zh = lax.rem(f // 2, 2)
    x = lax.rem(f // 4, 4)
    y = f // 16
    other = 1 - core

    def dev(r=rep, yy=y, xx=x, zz=zh, cc=core):
        return (r, ((yy * 4 + xx) * 2 + zz) * 2 + cc)

    def up(i, by=1):
        return lax.rem(i + by, 4)

    side = {
        "x": dict(me=x, r=dev(xx=up(x)), l=dev(xx=up(x, 3))),
        "y": dict(me=y, r=dev(yy=up(y)), l=dev(yy=up(y, 3))),
    }

    def axis_of(half, phase):
        return side["x" if half == phase else "y"]

    def axis_rs(half, phase):
        return side["x" if half == phase else "y"]

    def rc(src, dst, c, k, where):
        return pltpu.make_async_remote_copy(
            src_ref=src, dst_ref=dst, send_sem=ssem.at[c, k], recv_sem=rsem.at[c, k],
            device_id=where, device_id_type=MESH)

    my_rows = pl.ds(m16(core * TOK, TOK), TOK)
    my_cols = pl.ds(m16(core * 1024, 1024), 1024)
    other_cols = pl.ds(m16(other * 1024, 1024), 1024)
    loads = [
        pltpu.make_async_copy(p_h.at[0], b["p"], lsem.at[0]),
        pltpu.make_async_copy(m_h.at[0], b["m"], lsem.at[1]),
        pltpu.make_async_copy(tok_h.at[0], b["tok"].at[my_rows, :], lsem.at[2]),
        pltpu.make_async_copy(q_h.at[0, :, my_cols], b["q"].at[my_rows, :], lsem.at[3]),
        pltpu.make_async_copy(cot_h.at[0, :, my_cols], b["cot"].at[my_rows, :], lsem.at[4]),
    ]
    for load in loads:
        load.start()

    barrier = pltpu.get_barrier_semaphore()
    partners = [dev(cc=other), dev(zz=1 - zh), dev(zz=1 - zh, cc=other)]
    partners += [side[a][d] for a in ("x", "y") for d in ("r", "l")]
    partners += [dev(r=up(rep, d), cc=cc) for d in (1, 2, 3) for cc in (core, other)]
    for partner in partners:
        pl.semaphore_signal(barrier, inc=1, device_id=partner, device_id_type=MESH)

    loads[0].wait()
    for c in range(CH):
        for d in range(2):
            k0 = d * 512 + c * 128
            v = jnp.concatenate([b["p"][:, k0:k0 + 128], b["p"][:, 1024 + k0:1024 + k0 + 128]], axis=1)
            v = jnp.concatenate([v, jnp.zeros((12, 256), F32)], axis=0)
            b["piece"][c, d] = v.astype(BF16)

    pl.semaphore_wait(barrier, len(partners))

    quad = [(dev(cc=other), zh * 2 + other, other),
            (dev(zz=1 - zh), (1 - zh) * 2 + core, core),
            (dev(zz=1 - zh, cc=other), (1 - zh) * 2 + other, other)]
    my_slot = zh * 2 + core

    def quad_send(c):
        for k, (where, _, d) in enumerate(quad):
            rc(b["piece"].at[c, d], b["pin"].at[c, my_slot], c, M_QUAD + k, where).start()

    def quad_done(c):
        for k, (where, slot, d) in enumerate(quad):
            rc(b["piece"].at[c, d], b["pin"].at[c, slot], c, M_QUAD + k, where).wait_recv()
        b["pin"][c, my_slot] = b["piece"][c, core]
        v = [b["pin"][c, s].astype(F32)[:OWN] for s in range(4)]
        b["w"][c, y, pl.ds(m16(x * ROWS), ROWS), :] = jnp.concatenate(v, axis=0).astype(BF16)

    def w_unit(c, half, phase, j, part):
        lanes = pl.ds(half * 128, 128)
        w = b["w"]
        if phase == 0:
            at, n = dict(all=(0, ROWS), p=(0, 80), q=(80, 64))[part]
            if half == 0:
                return w.at[c, y, pl.ds(m16(j * ROWS + at), n), lanes]
            return w.at[c, j, pl.ds(m16(x * ROWS + at), n), lanes]
        if half == 0:
            at, n = dict(all=(0, 576), p=(0, 288), q=(288, 288))[part]
            return w.at[c, j, pl.ds(at, n), lanes]
        at, n = dict(all=(0, 4), p=(0, 2), q=(2, 2))[part]
        return w.at[c, pl.ds(at, n), pl.ds(m16(j * ROWS), ROWS), lanes]

    def ag_copy(c, half, phase, k, j):
        s = axis_of(half, phase)
        unit = w_unit(c, half, phase, j, ("all", "all", "p", "q")[k])
        return rc(unit, unit, c, M_AG + half * 8 + phase * 4 + k, s["r"] if k % 2 == 0 else s["l"])

    def ag_start(c, half, phase):
        me = axis_of(half, phase)["me"]
        ag_copy(c, half, phase, 0, me).start()
        ag_copy(c, half, phase, 1, me).start()

    def ag_mid(c, half, phase):
        me = axis_of(half, phase)["me"]
        ag_copy(c, half, phase, 0, up(me, 3)).wait_recv()
        ag_copy(c, half, phase, 2, up(me, 3)).start()
        ag_copy(c, half, phase, 1, up(me)).wait_recv()
        ag_copy(c, half, phase, 3, up(me)).start()

    def ag_end(c, half, phase):
        me = axis_of(half, phase)["me"]
        ag_copy(c, half, phase, 2, up(me, 2)).wait_recv()
        ag_copy(c, half, phase, 3, up(me, 2)).wait_recv()

    def transpose_rows(s):
        rows = pl.ds(m16(s * 256, 256), 256)

        def one(k, _):
            cols = pl.ds(m16(k * 256, 256), 256)
            b["tok_t"][cols, rows] = b["tok"][rows, cols].T
            return 0

        lax.fori_loop(0, D // 256, one, 0)

    causal = lax.broadcasted_iota(jnp.int32, (LENGTH, LENGTH), 0) <= lax.broadcasted_iota(
        jnp.int32, (LENGTH, LENGTH), 1)
    scale_in = D ** (-0.5)

    def nt(a, bb):
        return lax.dot_general(a, bb, (((1,), (1,)), ((), ())), preferred_element_type=F32)

    def attend(c, s):
        rows = pl.ds(m16(s * 256, 256), 256)
        w = b["w"][c].reshape(D, 256)
        joined = (jnp.dot(b["tok"][rows, :], w, preferred_element_type=F32) * scale_in).astype(BF16)
        key = joined[:, :HEAD].astype(F32)
        val = joined[:, HEAD:]
        cos, sin = cos_ref[...], sin_ref[...]
        rot = (key * cos + pltpu.roll(key, 64, 1) * sin).astype(BF16)
        d_val = jnp.zeros((LENGTH, HEAD), F32)
        d_rot = jnp.zeros((LENGTH, HEAD), F32)
        for head in range(2):
            cols = pl.ds(m16(c * 256 + head * 128, 128), 128)
            qh = b["q"][rows, cols]
            ch = b["cot"][rows, cols]
            bent = jnp.tanh(nt(rot, qh) * (SCORE_SCALE / SOFT_CAP))
            weights = jnp.where(causal, jnp.exp(SOFT_CAP * bent), 0.0)
            shares = weights * (1.0 / jnp.sum(weights, axis=0, keepdims=True))
            d_val += jnp.dot(shares.astype(BF16), ch, preferred_element_type=F32)
            share_grad = nt(val, ch)
            mean = jnp.sum(shares * share_grad, axis=0, keepdims=True)
            score = shares * (share_grad - mean) * ((1.0 - bent * bent) * SCORE_SCALE)
            d_rot += jnp.dot(score.astype(BF16), qh, preferred_element_type=F32)
        d_key = d_rot * cos - pltpu.roll(d_rot, 64, 1) * sin
        b["grads"][rows, :] = (jnp.concatenate([d_key, d_val], axis=1) * scale_in).astype(BF16)

    def gradient(c, yy):
        rows = pl.ds(m16(yy * 576, 64), 576)
        v = jnp.dot(b["tok_t"][rows, :], b["grads"][...], preferred_element_type=F32)
        b["f"][c, yy] = v
        b["g"][c, yy] = v.astype(BF16)

    def unit(name, c, half, phase, j, part):
        if phase == 0:
            ref = b["f" if name == "f" else "g"]
            if half == 0:
                return ref.at[c, pl.ds(0 if part == "p" else 2, 2), pl.ds(m16(j * ROWS), ROWS), pl.ds(0, 128)]
            return ref.at[c, j, pl.ds(0 if part == "p" else 288, 288), pl.ds(128, 128)]
        ref = b["h" if name == "f" else "hb"]
        return ref.at[c, half, j, pl.ds(0, 80) if part == "p" else pl.ds(80, 64), :]

    def buf(c, half, phase, name):
        return b["xy"[phase] + str(half) + name].at[c]

    RS_DST = ("al", "ar", "bl", "br", "cl", "cr")
    RS_PART = ("p", "q", "q", "p", "p", "q")

    def rs_copy(c, half, phase, k):
        s = axis_rs(half, phase)
        me = s["me"]
        if k < 4:
            j = (up(me, 2), up(me, 2), up(me), up(me, 3))[k]
            src = unit("g", c, half, phase, j, RS_PART[k])
        else:
            src = buf(c, half, phase, "tr" if k == 4 else "tl")
        return rc(src, buf(c, half, phase, RS_DST[k]), c, M_RS + half * 12 + phase * 6 + k,
                  s["r"] if k % 2 == 0 else s["l"])

    def rs_start(c, half, phase):
        for k in range(4):
            rs_copy(c, half, phase, k).start()

    def rs_mid(c, half, phase):
        me = axis_rs(half, phase)["me"]
        for k, j, part, arrived, out in ((0, up(me), "p", "al", "tr"), (1, up(me, 3), "q", "ar", "tl")):
            rs_copy(c, half, phase, k).wait_recv()
            total = unit("f", c, half, phase, j, part)[...] + buf(c, half, phase, arrived)[...].astype(F32)
            buf(c, half, phase, out)[...] = total.astype(BF16)
            rs_copy(c, half, phase, 4 + k).start()

    def rs_end(c, half, phase):
        me = axis_rs(half, phase)["me"]
        for k in range(2, 6):
            rs_copy(c, half, phase, k).wait_recv()
        for part, one, two in (("p", "cl", "br"), ("q", "bl", "cr")):
            total = (unit("f", c, half, phase, me, part)[...]
                     + buf(c, half, phase, one)[...].astype(F32) + buf(c, half, phase, two)[...].astype(F32))
            if phase == 0:
                at = pl.ds(0 if part == "p" else 2, 2)
                total = total.reshape(2, ROWS, 128)
                b["h"][c, half, at] = total
                b["hb"][c, half, at] = total.astype(BF16)
            else:
                at = pl.ds(0, 80) if part == "p" else pl.ds(80, 64)
                b["e"][c, at, pl.ds(half * 128, 128)] = total

    def z_copy(c):
        return rc(b["zs"].at[c], b["zr"].at[c], c, M_Z, dev(zz=1 - zh))

    def z_send(c):
        v = b["e"][c]
        b["zs"][c] = jnp.where(zh == 0, v[64:], v[:80]).astype(BF16)
        z_copy(c).start()

    def fix_copy(c, slot):
        return rc(b["fs"].at[c], b["gx"].at[c, slot], c, M_FIX, dev(cc=other))

    def gossip_copy(c, distance, rel, slot):
        to = core if rel == 0 else other
        return rc(b["gb"].at[c, to], b["gp"].at[distance - 1, c, slot], c,
                  M_GOS + (distance - 1) * 2 + rel, dev(r=up(rep, distance), cc=to))

    def z_done(c):
        z_copy(c).wait_recv()
        v = b["e"][c]
        r = b["zr"][c].astype(F32)
        total = jnp.where(zh == 0, v[:72], v[72:]) + jnp.where(zh == 0, r[:72], r[8:])
        first, last = total[:40], total[32:]
        b["gx"][c, core] = jnp.where(core == 0, first, last)
        b["fs"][c] = jnp.where(core == 0, last, first)
        b["gb"][c, 0] = total[:48].astype(BF16)
        b["gb"][c, 1] = total[24:].astype(BF16)
        for distance in (1, 2):
            for rel in (0, 1):
                gossip_copy(c, distance, rel, core).start()
        fix_copy(c, core).start()

    t = step_ref[0]
    learn_now = LEARN_RATE * (t.astype(F32) + 1.0) / WARM_SPAN
    near = lax.rem(t, 2) == 0

    def finish(c):
        fix_copy(c, other).wait_recv()
        for distance in (1, 2):
            for rel in (0, 1):
                gossip_copy(c, distance, rel, core if rel == 0 else other).wait_recv()
        for d in range(2):
            own = b["gx"][c, d]
            own = jnp.where(core == 0, own[:OWN], own[4:])
            peer = jnp.where(near, b["gp"][0, c, d], b["gp"][1, c, d]).astype(F32)
            peer = jnp.where(core == 0, peer[:OWN], peer[12:])
            for kv in range(2):
                cols = pl.ds(m16(kv * 1024 + d * 512 + c * 128, 128), 128)
                lanes = slice(kv * 128, kv * 128 + 128)
                peer_p = jnp.where(near, b["peer"][0, 0, :, cols], b["peer"][1, 0, :, cols])
                peer_m = jnp.where(near, b["peer"][0, 1, :, cols], b["peer"][1, 1, :, cols])
                mom = MOMENTUM_DECAY * b["m"][:, cols] + own[:, lanes]
                mom2 = MOMENTUM_DECAY * peer_m + peer[:, lanes]
                outm_ref[:, cols] = mom + mom2
                outp_ref[:, cols] = (b["p"][:, cols] - learn_now * mom) + (peer_p - learn_now * mom2)

    def exchange(k, slot):
        src = (tok_h.at[0], q_h.at[0, :, other_cols], cot_h.at[0, :, other_cols])[k]
        dst = b[("tok", "q", "cot")[k]].at[pl.ds(m16(slot * TOK, TOK), TOK), :]
        return pltpu.make_async_remote_copy(
            src_ref=src, dst_ref=dst, send_sem=gssem.at[k], recv_sem=grsem.at[k],
            device_id=dev(cc=other), device_id_type=MESH)

    def peer_copy(distance, k):
        at = 3 + (distance - 1) * 2 + k
        return pltpu.make_async_remote_copy(
            src_ref=(p_h, m_h)[k].at[0], dst_ref=b["peer"].at[distance - 1, k], send_sem=gssem.at[at],
            recv_sem=grsem.at[at], device_id=dev(r=up(rep, distance)), device_id_type=MESH)

    def each(*steps):
        def body(c, _):
            for step in steps:
                step(c)
            return 0

        lax.fori_loop(0, CH, body, 0)

    def halves(step, phase):
        def run(c):
            step(c, 0, phase)
            step(c, 1, phase)

        return run

    each(quad_send)
    for k in range(3):
        exchange(k, core).start()
    each(quad_done, halves(ag_start, 0))
    for distance in (1, 2):
        for k in range(2):
            peer_copy(distance, k).start()
    loads[2].wait()
    transpose_rows(core * 2)
    each(halves(ag_mid, 0))
    transpose_rows(core * 2 + 1)
    each(halves(ag_end, 0), halves(ag_start, 1))
    exchange(0, other).wait_recv()
    transpose_rows(other * 2)
    transpose_rows(other * 2 + 1)
    each(halves(ag_mid, 1))
    for k in (1, 2):
        exchange(k, other).wait_recv()
    for k in (1, 3, 4):
        loads[k].wait()

    def work(c):
        halves(ag_end, 1)(c)
        lax.fori_loop(0, 4, lambda s, _: (attend(c, s), 0)[1], 0)
        lax.fori_loop(0, 4, lambda yy, _: (gradient(c, yy), 0)[1], 0)
        halves(rs_start, 0)(c)

        @pl.when(c > 0)
        def _():
            halves(rs_mid, 0)(c - 1)

    each(work)
    halves(rs_mid, 0)(CH - 1)
    each(halves(rs_end, 0), halves(rs_start, 1))
    each(halves(rs_mid, 1))
    each(halves(rs_end, 1), z_send)
    each(z_done)
    for distance in (1, 2):
        for k in range(2):
            peer_copy(distance, k).wait_recv()
    each(finish)

    def drain(c):
        for k, (where, _, d) in enumerate(quad):
            rc(b["piece"].at[c, d], b["pin"].at[c, my_slot], c, M_QUAD + k, where).wait_send()
        for half in range(2):
            for phase in range(2):
                for k in range(4):
                    ag_copy(c, half, phase, k, up(axis_of(half, phase)["me"], (0, 0, 3, 1)[k])).wait_send()
                for k in range(6):
                    rs_copy(c, half, phase, k).wait_send()
        z_copy(c).wait_send()
        fix_copy(c, core).wait_send()
        for distance in (1, 2):
            for rel in (0, 1):
                gossip_copy(c, distance, rel, core).wait_send()

    each(drain)
    for k in range(3):
        exchange(k, core).wait_send()
    for distance in (1, 2):
        for k in range(2):
            peer_copy(distance, k).wait_send()


def shards(step_index, tokens, queries, cotangent, params, momentum):
    cos, sin = rope_tables()
    anywhere = pl.BlockSpec(memory_space=pl.ANY)
    vmem = pl.BlockSpec(memory_space=pltpu.VMEM)
    sum_p, sum_m = pl.pallas_call(
        kernel,
        out_shape=[jax.ShapeDtypeStruct((OWN, WIDE), F32)] * 2,
        in_specs=[pl.BlockSpec(memory_space=pltpu.SMEM)] + [anywhere] * 5 + [vmem] * 2,
        out_specs=[vmem, vmem],
        scratch_shapes=[pltpu.VMEM(shape, dtype) for shape, dtype in SCRATCH.values()]
        + [
            pltpu.SemaphoreType.DMA((CH, M_ALL)),
            pltpu.SemaphoreType.DMA((CH, M_ALL)),
            pltpu.SemaphoreType.DMA((7,)),
            pltpu.SemaphoreType.DMA((7,)),
            pltpu.SemaphoreType.DMA((5,)),
        ],
        compiler_params=pltpu.CompilerParams(
            collective_id=0, has_side_effects=True, vmem_limit_bytes=60 * 2**20),
        cost_estimate=pl.CostEstimate(flops=13 * 10**9, bytes_accessed=10**7, transcendentals=4 * 10**6),
    )(step_index, tokens, queries, cotangent, params, momentum, jnp.asarray(cos), jnp.asarray(sin))
    return 0.5 * sum_p[None], 0.5 * sum_m[None]


def solution(mesh):
    rows = P("rep", "fsdp", None)
    return jax.shard_map(
        shards,
        mesh=mesh,
        in_specs=(P(), rows, rows, rows, rows, rows),
        out_specs=(rows, rows),
        check_vma=False,
    )
```

```python
import functools

import jax
import jax.numpy as jnp
import numpy as np
from jax import lax
from jax.experimental import pallas as pl
from jax.experimental.pallas import tpu as pltpu
from jax.sharding import PartitionSpec as P

MESH = pl.DeviceIdType.MESH
F32 = jnp.float32
BF16 = jnp.bfloat16

HEAD = 128
LENGTH = 256
SOFT_CAP = 50.0
SCORE_SCALE = 144.0 ** (-0.5)
ROPE_THETA = 10000.0
LEARN_RATE = 0.1
WARM_SPAN = 64.0
MOMENTUM_DECAY = 0.9

D = 2304
TOK = 512
CH = 4
ROWS = 144
OWN = 36
WIDE = 2048
BLOCKS = WIDE // 128
LINES = OWN * BLOCKS

M_QUAD = 0
M_AG = 3
M_RS = 19
M_Z = 43
M_FIX = 44
M_GOS = 45
M_ALL = 49


def rope_tables():
    half = HEAD // 2
    inverse = np.float32(ROPE_THETA) ** (-np.arange(half, dtype=np.float32) / np.float32(half))
    angles = np.arange(LENGTH, dtype=np.float32)[:, None] * inverse[None, :].astype(np.float32)
    cos, sin = np.cos(angles), np.sin(angles)
    cos_full = np.concatenate([cos, cos], axis=1).astype(np.float32)
    sin_signed = np.concatenate([-sin, sin], axis=1).astype(np.float32)
    return cos_full, sin_signed


def m16(value, by=16):
    return pl.multiple_of(value, by)


SCRATCH = dict(
    tok=((2 * TOK, D), BF16),
    tok_t=((D, 2 * TOK), BF16),
    q=((2 * TOK, 1024), BF16),
    cot=((2 * TOK, 1024), BF16),
    p=((LINES, 128), F32),
    m=((LINES, 128), F32),
    peer=((2, 2, LINES, 128), F32),
    piece=((CH, 2, 80, 128), BF16),
    pin=((CH, 4, 80, 128), BF16),
    w=((CH, 4, 576, 256), BF16),
    grads=((2 * TOK, 256), BF16),
    f=((CH, 4, 576, 256), F32),
    g=((CH, 4, 576, 256), BF16),
    h=((CH, 2, 4, ROWS, 128), F32),
    hb=((CH, 2, 4, ROWS, 128), BF16),
    e=((CH, ROWS, 256), F32),
    zs=((CH, 80, 256), BF16),
    zr=((CH, 80, 256), BF16),
    fs=((CH, 72, 128), F32),
    gx=((CH, 2, 72, 128), F32),
    gb=((CH, 2, 80, 128), BF16),
    gp=((2, CH, 2, 80, 128), BF16),
)
PARTS = ("al", "bl", "cl", "ar", "br", "cr", "tr", "tl")
P_PARTS = ("al", "cl", "br", "tr")
for _name in PARTS:
    SCRATCH["x0" + _name] = ((CH, 2, ROWS, 128), BF16)
    SCRATCH["x1" + _name] = ((CH, 288, 128), BF16)
    for _half in (0, 1):
        SCRATCH["y%d%s" % (_half, _name)] = ((CH, 80 if _name in P_PARTS else 64, 128), BF16)
NAMES = tuple(SCRATCH)


def kernel(step_ref, tok_h, q_h, cot_h, p_h, m_h, cos_ref, sin_ref, outp_ref, outm_ref, *scratch):
    b = dict(zip(NAMES, scratch))
    ssem, rsem, gssem, grsem, lsem = scratch[len(NAMES):]
    rep = lax.axis_index("rep")
    f = lax.axis_index("fsdp")
    core = lax.rem(f, 2)
    zh = lax.rem(f // 2, 2)
    x = lax.rem(f // 4, 4)
    y = f // 16
    other = 1 - core

    def dev(r=rep, yy=y, xx=x, zz=zh, cc=core):
        return (r, ((yy * 4 + xx) * 2 + zz) * 2 + cc)

    def up(i, by=1):
        return lax.rem(i + by, 4)

    side = {
        "x": dict(me=x, r=dev(xx=up(x)), l=dev(xx=up(x, 3))),
        "y": dict(me=y, r=dev(yy=up(y)), l=dev(yy=up(y, 3))),
    }

    def axis_of(half, phase):
        return side["x" if half == phase else "y"]

    def axis_rs(half, phase):
        return side["x" if half == phase else "y"]

    def rc(src, dst, c, k, where):
        return pltpu.make_async_remote_copy(
            src_ref=src, dst_ref=dst, send_sem=ssem.at[c, k], recv_sem=rsem.at[c, k],
            device_id=where, device_id_type=MESH)

    def strip(block):
        return pl.ds(block, OWN, stride=BLOCKS)

    my_rows = pl.ds(m16(core * TOK, TOK), TOK)
    my_cols = pl.ds(m16(core * 1024, 1024), 1024)
    other_cols = pl.ds(m16(other * 1024, 1024), 1024)
    loads = [
        pltpu.make_async_copy(p_h, b["p"], lsem.at[0]),
        pltpu.make_async_copy(m_h, b["m"], lsem.at[1]),
        pltpu.make_async_copy(tok_h.at[0], b["tok"].at[my_rows, :], lsem.at[2]),
        pltpu.make_async_copy(q_h.at[0, :, my_cols], b["q"].at[my_rows, :], lsem.at[3]),
        pltpu.make_async_copy(cot_h.at[0, :, my_cols], b["cot"].at[my_rows, :], lsem.at[4]),
    ]
    for load in loads:
        load.start()

    barrier = pltpu.get_barrier_semaphore()
    partners = [dev(cc=other), dev(zz=1 - zh), dev(zz=1 - zh, cc=other)]
    partners += [side[a][d] for a in ("x", "y") for d in ("r", "l")]
    partners += [dev(r=up(rep, d), cc=cc) for d in (1, 2, 3) for cc in (core, other)]
    for partner in partners:
        pl.semaphore_signal(barrier, inc=1, device_id=partner, device_id_type=MESH)

    loads[0].wait()
    for c in range(CH):
        for d in range(2):
            at = d * 4 + c
            v = [b["p"][strip(at), :], b["p"][strip(8 + at), :], jnp.zeros((8, 128), F32)]
            b["piece"][c, d] = jnp.concatenate(v, axis=0).astype(BF16)

    pl.semaphore_wait(barrier, len(partners))

    quad = [(dev(cc=other), zh * 2 + other, other),
            (dev(zz=1 - zh), (1 - zh) * 2 + core, core),
            (dev(zz=1 - zh, cc=other), (1 - zh) * 2 + other, other)]
    my_slot = zh * 2 + core

    def quad_send(c):
        for k, (where, _, d) in enumerate(quad):
            rc(b["piece"].at[c, d], b["pin"].at[c, my_slot], c, M_QUAD + k, where).start()

    def quad_done(c):
        for k, (where, slot, d) in enumerate(quad):
            rc(b["piece"].at[c, d], b["pin"].at[c, slot], c, M_QUAD + k, where).wait_recv()
        b["pin"][c, my_slot] = b["piece"][c, core]
        v = [b["pin"][c, s].astype(F32) for s in range(4)]
        for kv in range(2):
            block = jnp.concatenate([u[kv * OWN:(kv + 1) * OWN] for u in v], axis=0)
            b["w"][c, y, pl.ds(m16(x * ROWS), ROWS), pl.ds(kv * 128, 128)] = block.astype(BF16)

    def w_unit(c, half, phase, j, part):
        lanes = pl.ds(half * 128, 128)
        w = b["w"]
        if phase == 0:
            at, n = dict(all=(0, ROWS), p=(0, 80), q=(80, 64))[part]
            if half == 0:
                return w.at[c, y, pl.ds(m16(j * ROWS + at), n), lanes]
            return w.at[c, j, pl.ds(m16(x * ROWS + at), n), lanes]
        if half == 0:
            at, n = dict(all=(0, 576), p=(0, 288), q=(288, 288))[part]
            return w.at[c, j, pl.ds(at, n), lanes]
        at, n = dict(all=(0, 4), p=(0, 2), q=(2, 2))[part]
        return w.at[c, pl.ds(at, n), pl.ds(m16(j * ROWS), ROWS), lanes]

    def ag_copy(c, half, phase, k, j):
        s = axis_of(half, phase)
        unit = w_unit(c, half, phase, j, ("all", "all", "p", "q")[k])
        return rc(unit, unit, c, M_AG + half * 8 + phase * 4 + k, s["r"] if k % 2 == 0 else s["l"])

    def ag_start(c, half, phase):
        me = axis_of(half, phase)["me"]
        ag_copy(c, half, phase, 0, me).start()
        ag_copy(c, half, phase, 1, me).start()

    def ag_mid(c, half, phase):
        me = axis_of(half, phase)["me"]
        ag_copy(c, half, phase, 0, up(me, 3)).wait_recv()
        ag_copy(c, half, phase, 2, up(me, 3)).start()
        ag_copy(c, half, phase, 1, up(me)).wait_recv()
        ag_copy(c, half, phase, 3, up(me)).start()

    def ag_end(c, half, phase):
        me = axis_of(half, phase)["me"]
        ag_copy(c, half, phase, 2, up(me, 2)).wait_recv()
        ag_copy(c, half, phase, 3, up(me, 2)).wait_recv()

    def transpose_rows(s):
        rows = pl.ds(m16(s * 256, 256), 256)

        def one(k, _):
            cols = pl.ds(m16(k * 256, 256), 256)
            b["tok_t"][cols, rows] = b["tok"][rows, cols].T
            return 0

        lax.fori_loop(0, D // 256, one, 0)

    causal = lax.broadcasted_iota(jnp.int32, (LENGTH, LENGTH), 0) <= lax.broadcasted_iota(
        jnp.int32, (LENGTH, LENGTH), 1)
    scale_in = D ** (-0.5)

    def nt(a, bb):
        return lax.dot_general(a, bb, (((1,), (1,)), ((), ())), preferred_element_type=F32)

    def attend(c, s):
        rows = pl.ds(m16(s * 256, 256), 256)
        w = b["w"][c].reshape(D, 256)
        joined = (jnp.dot(b["tok"][rows, :], w, preferred_element_type=F32) * scale_in).astype(BF16)
        key = joined[:, :HEAD].astype(F32)
        val = joined[:, HEAD:]
        cos, sin = cos_ref[...], sin_ref[...]
        rot = (key * cos + pltpu.roll(key, 64, 1) * sin).astype(BF16)
        d_val = jnp.zeros((LENGTH, HEAD), F32)
        d_rot = jnp.zeros((LENGTH, HEAD), F32)
        for head in range(2):
            cols = pl.ds(m16(c * 256 + head * 128, 128), 128)
            qh = b["q"][rows, cols]
            ch = b["cot"][rows, cols]
            bent = jnp.tanh(nt(rot, qh) * (SCORE_SCALE / SOFT_CAP))
            weights = jnp.where(causal, jnp.exp(SOFT_CAP * bent), 0.0)
            shares = weights * (1.0 / jnp.sum(weights, axis=0, keepdims=True))
            d_val += jnp.dot(shares.astype(BF16), ch, preferred_element_type=F32)
            share_grad = nt(val, ch)
            mean = jnp.sum(shares * share_grad, axis=0, keepdims=True)
            score = shares * (share_grad - mean) * ((1.0 - bent * bent) * SCORE_SCALE)
            d_rot += jnp.dot(score.astype(BF16), qh, preferred_element_type=F32)
        d_key = d_rot * cos - pltpu.roll(d_rot, 64, 1) * sin
        b["grads"][rows, :] = (jnp.concatenate([d_key, d_val], axis=1) * scale_in).astype(BF16)

    def gradient(c, yy):
        rows = pl.ds(m16(yy * 576, 64), 576)
        v = jnp.dot(b["tok_t"][rows, :], b["grads"][...], preferred_element_type=F32)
        b["f"][c, yy] = v
        b["g"][c, yy] = v.astype(BF16)

    def unit(name, c, half, phase, j, part):
        if phase == 0:
            ref = b["f" if name == "f" else "g"]
            if half == 0:
                return ref.at[c, pl.ds(0 if part == "p" else 2, 2), pl.ds(m16(j * ROWS), ROWS), pl.ds(0, 128)]
            return ref.at[c, j, pl.ds(0 if part == "p" else 288, 288), pl.ds(128, 128)]
        ref = b["h" if name == "f" else "hb"]
        return ref.at[c, half, j, pl.ds(0, 80) if part == "p" else pl.ds(80, 64), :]

    def buf(c, half, phase, name):
        return b["xy"[phase] + str(half) + name].at[c]

    RS_DST = ("al", "ar", "bl", "br", "cl", "cr")
    RS_PART = ("p", "q", "q", "p", "p", "q")

    def rs_copy(c, half, phase, k):
        s = axis_rs(half, phase)
        me = s["me"]
        if k < 4:
            j = (up(me, 2), up(me, 2), up(me), up(me, 3))[k]
            src = unit("g", c, half, phase, j, RS_PART[k])
        else:
            src = buf(c, half, phase, "tr" if k == 4 else "tl")
        return rc(src, buf(c, half, phase, RS_DST[k]), c, M_RS + half * 12 + phase * 6 + k,
                  s["r"] if k % 2 == 0 else s["l"])

    def rs_start(c, half, phase):
        for k in range(4):
            rs_copy(c, half, phase, k).start()

    def rs_mid(c, half, phase):
        me = axis_rs(half, phase)["me"]
        for k, j, part, arrived, out in ((0, up(me), "p", "al", "tr"), (1, up(me, 3), "q", "ar", "tl")):
            rs_copy(c, half, phase, k).wait_recv()
            total = unit("f", c, half, phase, j, part)[...] + buf(c, half, phase, arrived)[...].astype(F32)
            buf(c, half, phase, out)[...] = total.astype(BF16)
            rs_copy(c, half, phase, 4 + k).start()

    def rs_end(c, half, phase):
        me = axis_rs(half, phase)["me"]
        for k in range(2, 6):
            rs_copy(c, half, phase, k).wait_recv()
        for part, one, two in (("p", "cl", "br"), ("q", "bl", "cr")):
            total = (unit("f", c, half, phase, me, part)[...]
                     + buf(c, half, phase, one)[...].astype(F32) + buf(c, half, phase, two)[...].astype(F32))
            if phase == 0:
                at = pl.ds(0 if part == "p" else 2, 2)
                total = total.reshape(2, ROWS, 128)
                b["h"][c, half, at] = total
                b["hb"][c, half, at] = total.astype(BF16)
            else:
                at = pl.ds(0, 80) if part == "p" else pl.ds(80, 64)
                b["e"][c, at, pl.ds(half * 128, 128)] = total

    def z_copy(c):
        return rc(b["zs"].at[c], b["zr"].at[c], c, M_Z, dev(zz=1 - zh))

    def z_send(c):
        v = b["e"][c]
        b["zs"][c] = jnp.where(zh == 0, v[64:], v[:80]).astype(BF16)
        z_copy(c).start()

    def fix_copy(c, slot):
        return rc(b["fs"].at[c], b["gx"].at[c, slot], c, M_FIX, dev(cc=other))

    def gossip_copy(c, distance, rel, slot):
        to = core if rel == 0 else other
        return rc(b["gb"].at[c, to], b["gp"].at[distance - 1, c, slot], c,
                  M_GOS + (distance - 1) * 2 + rel, dev(r=up(rep, distance), cc=to))

    def z_done(c):
        z_copy(c).wait_recv()
        v = b["e"][c]
        r = b["zr"][c].astype(F32)
        total = jnp.where(zh == 0, v[:72], v[72:]) + jnp.where(zh == 0, r[:72], r[8:])
        first, last = (jnp.concatenate([total[r:r + OWN, :128], total[r:r + OWN, 128:]], axis=0) for r in (0, OWN))
        pad = jnp.zeros((8, 128), F32)
        b["gb"][c, 0] = jnp.concatenate([first, pad], axis=0).astype(BF16)
        b["gb"][c, 1] = jnp.concatenate([last, pad], axis=0).astype(BF16)
        b["fs"][c] = jnp.where(core == 0, last, first)
        b["gx"][c, core] = jnp.where(core == 0, first, last)
        for distance in (1, 2):
            for rel in (0, 1):
                gossip_copy(c, distance, rel, core).start()
        fix_copy(c, core).start()

    t = step_ref[0]
    learn_now = LEARN_RATE * (t.astype(F32) + 1.0) / WARM_SPAN
    near = lax.rem(t, 2) == 0

    def finish(c):
        fix_copy(c, other).wait_recv()
        for distance in (1, 2):
            for rel in (0, 1):
                gossip_copy(c, distance, rel, core if rel == 0 else other).wait_recv()
        for d in range(2):
            own = b["gx"][c, d]
            peer = jnp.where(near, b["gp"][0, c, d], b["gp"][1, c, d]).astype(F32)
            for kv in range(2):
                at = strip(kv * 8 + d * 4 + c)
                peer_p = jnp.where(near, b["peer"][0, 0, at, :], b["peer"][1, 0, at, :])
                peer_m = jnp.where(near, b["peer"][0, 1, at, :], b["peer"][1, 1, at, :])
                mom = MOMENTUM_DECAY * b["m"][at, :] + own[kv * OWN:(kv + 1) * OWN]
                mom2 = MOMENTUM_DECAY * peer_m + peer[kv * OWN:(kv + 1) * OWN]
                outm_ref[at, :] = mom + mom2
                outp_ref[at, :] = (b["p"][at, :] - learn_now * mom) + (peer_p - learn_now * mom2)

    def exchange(k, slot):
        src = (tok_h.at[0], q_h.at[0, :, other_cols], cot_h.at[0, :, other_cols])[k]
        dst = b[("tok", "q", "cot")[k]].at[pl.ds(m16(slot * TOK, TOK), TOK), :]
        return pltpu.make_async_remote_copy(
            src_ref=src, dst_ref=dst, send_sem=gssem.at[k], recv_sem=grsem.at[k],
            device_id=dev(cc=other), device_id_type=MESH)

    def peer_copy(distance, k):
        at = 3 + (distance - 1) * 2 + k
        return pltpu.make_async_remote_copy(
            src_ref=(p_h, m_h)[k], dst_ref=b["peer"].at[distance - 1, k], send_sem=gssem.at[at],
            recv_sem=grsem.at[at], device_id=dev(r=up(rep, distance)), device_id_type=MESH)

    def each(*steps):
        def body(c, _):
            for step in steps:
                step(c)
            return 0

        lax.fori_loop(0, CH, body, 0)

    def halves(step, phase):
        def run(c):
            step(c, 0, phase)
            step(c, 1, phase)

        return run

    def when(condition, *steps):
        def run():
            for step, c in steps:
                step(c)

        pl.when(condition)(run)

    ag0s, ag0m, ag0e = (halves(step, 0) for step in (ag_start, ag_mid, ag_end))
    ag1s, ag1m, ag1e = (halves(step, 1) for step in (ag_start, ag_mid, ag_end))
    rs0s, rs0m, rs0e = (halves(step, 0) for step in (rs_start, rs_mid, rs_end))
    rs1s, rs1m, rs1e = (halves(step, 1) for step in (rs_start, rs_mid, rs_end))

    each(quad_send)
    for k in range(3):
        exchange(k, core).start()
    for c in range(2):
        quad_done(c)
        ag0s(c)
    loads[2].wait()
    ag0m(0)
    quad_done(2)
    ag0s(2)
    ag0e(0)
    ag1s(0)
    ag0m(1)
    transpose_rows(core * 2)
    quad_done(3)
    ag0s(3)
    ag0e(1)
    ag1s(1)
    for distance in (1, 2):
        for k in range(2):
            peer_copy(distance, k).start()
    transpose_rows(core * 2 + 1)
    ag1m(0)
    exchange(0, other).wait_recv()
    transpose_rows(other * 2)
    ag0m(2)
    transpose_rows(other * 2 + 1)
    ag0m(3)
    for k in (1, 2):
        exchange(k, other).wait_recv()
    for k in (1, 3, 4):
        loads[k].wait()

    def work(c):
        ag1e(c)
        attend(c, 0)
        when(c + 1 < CH, (ag1m, c + 1))
        attend(c, 1)
        when(c > 0, (rs0m, c - 1))
        when(c + 2 < CH, (ag0e, c + 2), (ag1s, c + 2))
        attend(c, 2)
        when(c > 1, (z_done, c - 2))
        attend(c, 3)
        when(c > 0, (rs0e, c - 1), (rs1s, c - 1))
        gradient(c, 0)
        gradient(c, 1)
        when(c > 0, (rs1m, c - 1))
        gradient(c, 2)
        gradient(c, 3)
        rs0s(c)
        when(c > 0, (rs1e, c - 1), (z_send, c - 1))

    each(work)
    last = CH - 1
    rs0m(last)
    z_done(last - 1)
    rs0e(last)
    rs1s(last)
    for distance in (1, 2):
        for k in range(2):
            peer_copy(distance, k).wait_recv()
    for c in range(last - 1):
        finish(c)
    rs1m(last)
    finish(last - 1)
    rs1e(last)
    z_send(last)
    z_done(last)
    finish(last)

    def drain(c):
        for k, (where, _, d) in enumerate(quad):
            rc(b["piece"].at[c, d], b["pin"].at[c, my_slot], c, M_QUAD + k, where).wait_send()
        for half in range(2):
            for phase in range(2):
                for k in range(4):
                    ag_copy(c, half, phase, k, up(axis_of(half, phase)["me"], (0, 0, 3, 1)[k])).wait_send()
                for k in range(6):
                    rs_copy(c, half, phase, k).wait_send()
        z_copy(c).wait_send()
        fix_copy(c, core).wait_send()
        for distance in (1, 2):
            for rel in (0, 1):
                gossip_copy(c, distance, rel, core).wait_send()

    each(drain)
    for k in range(3):
        exchange(k, core).wait_send()
    for distance in (1, 2):
        for k in range(2):
            peer_copy(distance, k).wait_send()


def shards(step_index, tokens, queries, cotangent, params, momentum):
    cos, sin = rope_tables()
    anywhere = pl.BlockSpec(memory_space=pl.ANY)
    vmem = pl.BlockSpec(memory_space=pltpu.VMEM)
    sum_p, sum_m = pl.pallas_call(
        kernel,
        out_shape=[jax.ShapeDtypeStruct((LINES, 128), F32)] * 2,
        in_specs=[pl.BlockSpec(memory_space=pltpu.SMEM)] + [anywhere] * 5 + [vmem] * 2,
        out_specs=[vmem, vmem],
        scratch_shapes=[pltpu.VMEM(shape, dtype) for shape, dtype in SCRATCH.values()]
        + [
            pltpu.SemaphoreType.DMA((CH, M_ALL)),
            pltpu.SemaphoreType.DMA((CH, M_ALL)),
            pltpu.SemaphoreType.DMA((7,)),
            pltpu.SemaphoreType.DMA((7,)),
            pltpu.SemaphoreType.DMA((5,)),
        ],
        compiler_params=pltpu.CompilerParams(
            collective_id=0, has_side_effects=True, vmem_limit_bytes=60 * 2**20),
        cost_estimate=pl.CostEstimate(flops=13 * 10**9, bytes_accessed=10**7, transcendentals=4 * 10**6),
    )(step_index, tokens, queries, cotangent, params.reshape(LINES, 128), momentum.reshape(LINES, 128),
      jnp.asarray(cos), jnp.asarray(sin))
    return (0.5 * sum_p).reshape(1, OWN, WIDE), (0.5 * sum_m).reshape(1, OWN, WIDE)


def solution(mesh):
    rows = P("rep", "fsdp", None)
    return jax.shard_map(
        shards,
        mesh=mesh,
        in_specs=(P(), rows, rows, rows, rows, rows),
        out_specs=(rows, rows),
        check_vma=False,
    )
```

```python
import functools

import jax
import jax.numpy as jnp
import numpy as np
from jax import lax
from jax.experimental import pallas as pl
from jax.experimental.pallas import tpu as pltpu
from jax.sharding import PartitionSpec as P

MESH = pl.DeviceIdType.MESH
F32 = jnp.float32
BF16 = jnp.bfloat16

HEAD = 128
LENGTH = 256
SOFT_CAP = 50.0
SCORE_SCALE = 144.0 ** (-0.5)
ROPE_THETA = 10000.0
LEARN_RATE = 0.1
WARM_SPAN = 64.0
MOMENTUM_DECAY = 0.9
LOG2E = 1.4426950408889634

D = 2304
TOK = 512
CH = 4
ROWS = 144
OWN = 36
WIDE = 2048
BLOCKS = WIDE // 128

M_QUAD = 0
M_AG = 3
M_RS = 19
M_Z = 43
M_FIX = 44
M_GOS = 45
M_ALL = 47


def rope_tables():
    half = HEAD // 2
    inverse = np.float32(ROPE_THETA) ** (-np.arange(half, dtype=np.float32) / np.float32(half))
    angles = np.arange(LENGTH, dtype=np.float32)[:, None] * inverse[None, :].astype(np.float32)
    cos, sin = np.cos(angles), np.sin(angles)
    cos_full = np.concatenate([cos, cos], axis=1).astype(np.float32)
    sin_signed = np.concatenate([-sin, sin], axis=1).astype(np.float32)
    return cos_full, sin_signed


def m16(value, by=16):
    return pl.multiple_of(value, by)


SCRATCH = dict(
    tok=((2 * TOK, D), BF16),
    tok_t=((D, 2 * TOK), BF16),
    q=((2 * TOK, 1024), BF16),
    cot=((2 * TOK, 1024), BF16),
    p=((BLOCKS, OWN, 128), F32),
    m=((BLOCKS, OWN, 128), F32),
    peer=((2, BLOCKS, OWN, 128), F32),
    out_p=((BLOCKS, OWN, 128), F32),
    out_m=((BLOCKS, OWN, 128), F32),
    cos=((LENGTH, HEAD), F32),
    sin=((LENGTH, HEAD), F32),
    piece=((CH, 2, 80, 128), BF16),
    pin=((CH, 4, 80, 128), BF16),
    w=((CH, 4, 576, 256), BF16),
    joined=((2 * TOK, 256), BF16),
    grads=((2 * TOK, 256), BF16),
    f=((CH, 4, 576, 256), F32),
    g=((CH, 4, 576, 256), BF16),
    h=((CH, 2, 4, ROWS, 128), F32),
    hb=((CH, 2, 4, ROWS, 128), BF16),
    e=((CH, ROWS, 256), F32),
    zs=((CH, 80, 256), BF16),
    zr=((CH, 80, 256), BF16),
    fs=((CH, 72, 128), F32),
    gx=((CH, 2, 72, 128), F32),
    gb=((CH, 2, 80, 128), BF16),
    gp=((CH, 2, 80, 128), BF16),
)
PARTS = ("al", "bl", "cl", "ar", "br", "cr", "tr", "tl")
P_PARTS = ("al", "cl", "br", "tr")
for _name in PARTS:
    SCRATCH["x0" + _name] = ((CH, 2, ROWS, 128), BF16)
    SCRATCH["x1" + _name] = ((CH, 288, 128), BF16)
    for _half in (0, 1):
        SCRATCH["y%d%s" % (_half, _name)] = ((CH, 80 if _name in P_PARTS else 64, 128), BF16)
NAMES = tuple(SCRATCH)


def kernel(distance, step_ref, tok_h, q_h, cot_h, p_h, m_h, cos_h, sin_h, outp_h, outm_h, *scratch):
    b = dict(zip(NAMES, scratch))
    ssem, rsem, gssem, grsem, lsem, psem, osem = scratch[len(NAMES):]
    rep = lax.axis_index("rep")
    f = lax.axis_index("fsdp")
    core = lax.rem(f, 2)
    zh = lax.rem(f // 2, 2)
    x = lax.rem(f // 4, 4)
    y = f // 16
    other = 1 - core

    def dev(r=rep, yy=y, xx=x, zz=zh, cc=core):
        return (r, ((yy * 4 + xx) * 2 + zz) * 2 + cc)

    def up(i, by=1):
        return lax.rem(i + by, 4)

    side = {
        "x": dict(me=x, r=dev(xx=up(x)), l=dev(xx=up(x, 3))),
        "y": dict(me=y, r=dev(yy=up(y)), l=dev(yy=up(y, 3))),
    }

    def axis_of(half, phase):
        return side["x" if half == phase else "y"]

    def axis_rs(half, phase):
        return side["x" if half == phase else "y"]

    def rc(src, dst, c, k, where):
        return pltpu.make_async_remote_copy(
            src_ref=src, dst_ref=dst, send_sem=ssem.at[c, k], recv_sem=rsem.at[c, k],
            device_id=where, device_id_type=MESH)

    my_rows = pl.ds(m16(core * TOK, TOK), TOK)
    my_cols = pl.ds(m16(core * 1024, 1024), 1024)
    other_cols = pl.ds(m16(other * 1024, 1024), 1024)
    loads = [
        pltpu.make_async_copy(tok_h.at[0], b["tok"].at[my_rows, :], lsem.at[2]),
        pltpu.make_async_copy(q_h.at[0, :, my_cols], b["q"].at[my_rows, :], lsem.at[3]),
        pltpu.make_async_copy(cot_h.at[0, :, my_cols], b["cot"].at[my_rows, :], lsem.at[4]),
    ]
    loads += [
        pltpu.make_async_copy(cos_h, b["cos"], lsem.at[0]),
        pltpu.make_async_copy(sin_h, b["sin"], lsem.at[1]),
    ]
    strips = [[pltpu.make_async_copy(ref.at[:, k, :], b["pm"[i]].at[k], psem.at[i, k]) for k in range(BLOCKS)]
              for i, ref in enumerate((p_h, m_h))]
    order = [kd + c for c in range(CH) for kd in (0, 4, 8, 12)]
    for k in order:
        strips[0][k].start()
    for load in loads:
        load.start()
    for k in order:
        strips[1][k].start()

    barrier = pltpu.get_barrier_semaphore()
    partners = [dev(cc=other), dev(zz=1 - zh), dev(zz=1 - zh, cc=other)]
    partners += [side[a][d] for a in ("x", "y") for d in ("r", "l")]
    partners += [dev(xx=up(x, 2)), dev(yy=up(y, 2))]
    partners += [dev(r=up(rep, d), cc=cc) for d in sorted({distance, 4 - distance}) for cc in (core, other)]
    for partner in partners:
        pl.semaphore_signal(barrier, inc=1, device_id=partner, device_id_type=MESH)

    def make_pieces(c):
        for kd in (0, 4, 8, 12):
            strips[0][kd + c].wait()
        for d in range(2):
            v = [b["p"][d * 4 + c], b["p"][8 + d * 4 + c], jnp.zeros((8, 128), F32)]
            b["piece"][c, d] = jnp.concatenate(v, axis=0).astype(BF16)

    quad = [(dev(cc=other), zh * 2 + other, other),
            (dev(zz=1 - zh), (1 - zh) * 2 + core, core),
            (dev(zz=1 - zh, cc=other), (1 - zh) * 2 + other, other)]
    my_slot = zh * 2 + core

    def quad_send(c):
        for k, (where, _, d) in enumerate(quad):
            rc(b["piece"].at[c, d], b["pin"].at[c, my_slot], c, M_QUAD + k, where).start()

    def quad_done(c):
        for k, (where, slot, d) in enumerate(quad):
            rc(b["piece"].at[c, d], b["pin"].at[c, slot], c, M_QUAD + k, where).wait_recv()
        b["pin"][c, my_slot] = b["piece"][c, core]
        v = [b["pin"][c, s].astype(F32) for s in range(4)]
        for kv in range(2):
            block = jnp.concatenate([u[kv * OWN:(kv + 1) * OWN] for u in v], axis=0)
            b["w"][c, y, pl.ds(m16(x * ROWS), ROWS), pl.ds(kv * 128, 128)] = block.astype(BF16)

    def w_unit(c, half, phase, j, part):
        lanes = pl.ds(half * 128, 128)
        w = b["w"]
        if phase == 0:
            at, n = dict(all=(0, ROWS), p=(0, 80), q=(80, 64))[part]
            if half == 0:
                return w.at[c, y, pl.ds(m16(j * ROWS + at), n), lanes]
            return w.at[c, j, pl.ds(m16(x * ROWS + at), n), lanes]
        if half == 0:
            at, n = dict(all=(0, 576), p=(0, 288), q=(288, 288))[part]
            return w.at[c, j, pl.ds(at, n), lanes]
        at, n = dict(all=(0, 4), p=(0, 2), q=(2, 2))[part]
        return w.at[c, pl.ds(at, n), pl.ds(m16(j * ROWS), ROWS), lanes]

    def far(half, phase):
        return dev(xx=up(x, 2)) if half == phase else dev(yy=up(y, 2))

    def ag_copy(c, half, phase, k, j):
        s = axis_of(half, phase)
        unit = w_unit(c, half, phase, j, ("all", "all", "p", "q")[k])
        return rc(unit, unit, c, M_AG + half * 8 + phase * 4 + k, s["r"] if k % 2 == 0 else s["l"])

    def ag_start(c, half, phase):
        me = axis_of(half, phase)["me"]
        ag_copy(c, half, phase, 0, me).start()
        ag_copy(c, half, phase, 1, me).start()

    def ag_mid(c, half, phase):
        me = axis_of(half, phase)["me"]
        ag_copy(c, half, phase, 0, up(me, 3)).wait_recv()
        ag_copy(c, half, phase, 2, up(me, 3)).start()
        ag_copy(c, half, phase, 1, up(me)).wait_recv()
        ag_copy(c, half, phase, 3, up(me)).start()

    def ag_end(c, half, phase):
        me = axis_of(half, phase)["me"]
        ag_copy(c, half, phase, 2, up(me, 2)).wait_recv()
        ag_copy(c, half, phase, 3, up(me, 2)).wait_recv()

    def transpose_rows(s):
        rows = pl.ds(m16(s * 256, 256), 256)

        def one(k, _):
            cols = pl.ds(m16(k * 256, 256), 256)
            b["tok_t"][cols, rows] = b["tok"][rows, cols].T
            return 0

        lax.fori_loop(0, D // 256, one, 0)

    half_len = LENGTH // 2
    triangle = lax.broadcasted_iota(jnp.int32, (half_len, LENGTH), 0) <= lax.rem(
        lax.broadcasted_iota(jnp.int32, (half_len, LENGTH), 1), half_len)
    scale_in = D ** (-0.5)

    def nt(a, bb):
        return lax.dot_general(a, bb, (((1,), (1,)), ((), ())), preferred_element_type=F32)

    def project(c):
        w = b["w"][c].reshape(D, 256)
        b["joined"][...] = (jnp.dot(b["tok"][...], w, preferred_element_type=F32) * scale_in).astype(BF16)

    def attend(c, s):
        rows = pl.ds(m16(s * 256, 256), 256)
        joined = b["joined"][rows, :]
        key = joined[:, :HEAD].astype(F32)
        val = joined[:, HEAD:]
        cos, sin = b["cos"][...], b["sin"][...]
        rot = (key * cos + pltpu.roll(key, 64, 1) * sin).astype(BF16)
        d_val, d_rot = [], []
        for block in range(2):
            at = pl.ds(m16(s * LENGTH + block * half_len, half_len), half_len)
            cols = [pl.ds(m16(c * 256 + head * 128, 128), 128) for head in range(2)]
            qh = jnp.concatenate([b["q"][at, col] for col in cols], axis=0)
            ch = jnp.concatenate([b["cot"][at, col] for col in cols], axis=0)
            keys = half_len * (block + 1)
            bent = jnp.tanh(nt(rot[:keys], qh) * (SCORE_SCALE / SOFT_CAP))
            weights = jnp.exp2(bent * (SOFT_CAP * LOG2E))
            masked = jnp.where(triangle, weights[keys - half_len:], 0.0)
            weights = masked if block == 0 else jnp.concatenate([weights[:half_len], masked], axis=0)
            shares = weights * (1.0 / jnp.sum(weights, axis=0, keepdims=True))
            d_val.append(jnp.dot(shares.astype(BF16), ch, preferred_element_type=F32))
            share_grad = nt(val[:keys], ch)
            mean = jnp.sum(shares * share_grad, axis=0, keepdims=True)
            score = shares * (share_grad - mean) * (SCORE_SCALE - bent * bent * SCORE_SCALE)
            d_rot.append(jnp.dot(score.astype(BF16), qh, preferred_element_type=F32))
        d_val, d_rot = (jnp.concatenate([hi[:half_len] + lo, hi[half_len:]], axis=0) for lo, hi in (d_val, d_rot))
        d_key = d_rot * cos - pltpu.roll(d_rot, 64, 1) * sin
        b["grads"][rows, :] = (jnp.concatenate([d_key, d_val], axis=1) * scale_in).astype(BF16)

    def gradient(c, part):
        rows = pl.ds(m16(part * 1152, 128), 1152)
        v = jnp.dot(b["tok_t"][rows, :], b["grads"][...], preferred_element_type=F32).reshape(2, 576, 256)
        at = pl.ds(part * 2, 2)
        b["f"][c, at] = v
        b["g"][c, at] = v.astype(BF16)

    def unit(name, c, half, phase, j, part):
        if phase == 0:
            ref = b["f" if name == "f" else "g"]
            if half == 0:
                return ref.at[c, pl.ds(0 if part == "p" else 2, 2), pl.ds(m16(j * ROWS), ROWS), pl.ds(0, 128)]
            return ref.at[c, j, pl.ds(0 if part == "p" else 288, 288), pl.ds(128, 128)]
        ref = b["h" if name == "f" else "hb"]
        return ref.at[c, half, j, pl.ds(0, 80) if part == "p" else pl.ds(80, 64), :]

    def buf(c, half, phase, name):
        return b["xy"[phase] + str(half) + name].at[c]

    RS_DST = ("al", "ar", "bl", "br", "cl", "cr")
    RS_PART = ("p", "q", "q", "p", "p", "q")

    def rs_copy(c, half, phase, k):
        s = axis_rs(half, phase)
        me = s["me"]
        if k < 4:
            j = (up(me, 2), up(me, 2), up(me), up(me, 3))[k]
            src = unit("g", c, half, phase, j, RS_PART[k])
        else:
            src = buf(c, half, phase, "tr" if k == 4 else "tl")
        return rc(src, buf(c, half, phase, RS_DST[k]), c, M_RS + half * 12 + phase * 6 + k,
                  s["r"] if k % 2 == 0 else s["l"])

    def rs_start(c, half, phase):
        for k in range(4):
            rs_copy(c, half, phase, k).start()

    def rs_mid(c, half, phase):
        me = axis_rs(half, phase)["me"]
        for k, j, part, arrived, out in ((0, up(me), "p", "al", "tr"), (1, up(me, 3), "q", "ar", "tl")):
            rs_copy(c, half, phase, k).wait_recv()
            total = unit("f", c, half, phase, j, part)[...] + buf(c, half, phase, arrived)[...].astype(F32)
            buf(c, half, phase, out)[...] = total.astype(BF16)
            rs_copy(c, half, phase, 4 + k).start()

    def rs_end(c, half, phase):
        me = axis_rs(half, phase)["me"]
        for k in range(2, 6):
            rs_copy(c, half, phase, k).wait_recv()
        for part, one, two in (("p", "cl", "br"), ("q", "bl", "cr")):
            total = (unit("f", c, half, phase, me, part)[...]
                     + buf(c, half, phase, one)[...].astype(F32) + buf(c, half, phase, two)[...].astype(F32))
            if phase == 0:
                at = pl.ds(0 if part == "p" else 2, 2)
                total = total.reshape(2, ROWS, 128)
                b["h"][c, half, at] = total
                b["hb"][c, half, at] = total.astype(BF16)
            else:
                at = pl.ds(0, 80) if part == "p" else pl.ds(80, 64)
                b["e"][c, at, pl.ds(half * 128, 128)] = total

    def z_copy(c):
        return rc(b["zs"].at[c], b["zr"].at[c], c, M_Z, dev(zz=1 - zh))

    def z_send(c):
        v = b["e"][c]
        b["zs"][c] = jnp.where(zh == 0, v[64:], v[:80]).astype(BF16)
        z_copy(c).start()

    def fix_copy(c, slot):
        return rc(b["fs"].at[c], b["gx"].at[c, slot], c, M_FIX, dev(cc=other))

    def gossip_copy(c, rel, slot):
        to = core if rel == 0 else other
        return rc(b["gb"].at[c, to], b["gp"].at[c, slot], c, M_GOS + rel,
                  dev(r=up(rep, distance), cc=to))

    def z_done(c):
        z_copy(c).wait_recv()
        v = b["e"][c]
        r = b["zr"][c].astype(F32)
        total = jnp.where(zh == 0, v[:72], v[72:]) + jnp.where(zh == 0, r[:72], r[8:])
        first, last = (jnp.concatenate([total[r:r + OWN, :128], total[r:r + OWN, 128:]], axis=0) for r in (0, OWN))
        pad = jnp.zeros((8, 128), F32)
        b["gb"][c, 0] = jnp.concatenate([first, pad], axis=0).astype(BF16)
        b["gb"][c, 1] = jnp.concatenate([last, pad], axis=0).astype(BF16)
        b["fs"][c] = jnp.where(core == 0, last, first)
        b["gx"][c, core] = jnp.where(core == 0, first, last)
        for rel in (0, 1):
            gossip_copy(c, rel, core).start()
        fix_copy(c, core).start()

    t = step_ref[0]
    learn_now = LEARN_RATE * (t.astype(F32) + 1.0) / WARM_SPAN

    def out_copy(i, k):
        return pltpu.make_async_copy(b[("out_p", "out_m")[i]].at[k], (outp_h, outm_h)[i].at[:, k, :], osem.at[i, k])

    def finish(c):
        fix_copy(c, other).wait_recv()
        for rel in (0, 1):
            gossip_copy(c, rel, core if rel == 0 else other).wait_recv()
        for d in range(2):
            own = b["gx"][c, d]
            peer = b["gp"][c, d].astype(F32)
            for kv in range(2):
                at = kv * 8 + d * 4 + c
                mom = MOMENTUM_DECAY * b["m"][at] + own[kv * OWN:(kv + 1) * OWN]
                mom2 = MOMENTUM_DECAY * b["peer"][1, at] + peer[kv * OWN:(kv + 1) * OWN]
                b["out_m"][at] = mom + mom2
                b["out_p"][at] = (b["p"][at] - learn_now * mom) + (b["peer"][0, at] - learn_now * mom2)
                for i in range(2):
                    out_copy(i, at).start()

    def exchange(k, slot):
        src = (tok_h.at[0], q_h.at[0, :, other_cols], cot_h.at[0, :, other_cols])[k]
        dst = b[("tok", "q", "cot")[k]].at[pl.ds(m16(slot * TOK, TOK), TOK), :]
        return pltpu.make_async_remote_copy(
            src_ref=src, dst_ref=dst, send_sem=gssem.at[k], recv_sem=grsem.at[k],
            device_id=dev(cc=other), device_id_type=MESH)

    def peer_copy(k):
        at = 3 + k
        return pltpu.make_async_remote_copy(
            src_ref=b["pm"[k]], dst_ref=b["peer"].at[k], send_sem=gssem.at[at],
            recv_sem=grsem.at[at], device_id=dev(r=up(rep, distance)), device_id_type=MESH)

    def each(*steps):
        def body(c, _):
            for step in steps:
                step(c)
            return 0

        lax.fori_loop(0, CH, body, 0)

    def halves(step, phase):
        def run(c):
            step(c, 0, phase)
            step(c, 1, phase)

        return run

    def agd_copy(c, half, phase, k, j):
        s = axis_of(half, phase)
        block = w_unit(c, half, phase, j, "all")
        return rc(block, block, c, M_AG + half * 8 + phase * 4 + k, (s["r"], s["l"], far(half, phase))[k])

    def agd_start(c, half, phase):
        me = axis_of(half, phase)["me"]
        for k in (2, 0, 1):
            agd_copy(c, half, phase, k, me).start()

    def agd_end(c, half, phase):
        me = axis_of(half, phase)["me"]
        for k, by in ((0, 3), (1, 1), (2, 2)):
            agd_copy(c, half, phase, k, up(me, by)).wait_recv()

    def rsd_copy(c, half, phase, k, part):
        s = axis_rs(half, phase)
        me = s["me"]
        j = (up(me), up(me, 3), up(me, 2))[k]
        src = unit("g", c, half, phase, j, part)
        name = {"p": ("al", "br", "cl"), "q": ("ar", "bl", "cr")}[part][k]
        return rc(src, buf(c, half, phase, name), c, M_RS + half * 12 + phase * 6 + k * 2 + (part == "q"),
                  (s["r"], s["l"], far(half, phase))[k])

    def rsd_start(c, half, phase):
        for k in (2, 0, 1):
            for part in ("p", "q"):
                rsd_copy(c, half, phase, k, part).start()

    def rsd_end(c, half, phase):
        me = axis_rs(half, phase)["me"]
        for part in ("p", "q"):
            for k in range(3):
                rsd_copy(c, half, phase, k, part).wait_recv()
        for part, names in (("p", ("al", "br", "cl")), ("q", ("ar", "bl", "cr"))):
            total = unit("f", c, half, phase, me, part)[...]
            for name in names:
                total += buf(c, half, phase, name)[...].astype(F32)
            if phase == 0:
                at = pl.ds(0 if part == "p" else 2, 2)
                total = total.reshape(2, ROWS, 128)
                b["h"][c, half, at] = total
                b["hb"][c, half, at] = total.astype(BF16)
            else:
                at = pl.ds(0, 80) if part == "p" else pl.ds(80, 64)
                b["e"][c, at, pl.ds(half * 128, 128)] = total

    agd0s, agd0e = (halves(step, 0) for step in (agd_start, agd_end))
    ag1s, ag1m, ag1e = (halves(step, 1) for step in (ag_start, ag_mid, ag_end))
    rs0s, rs0m, rs0e = (halves(step, 0) for step in (rs_start, rs_mid, rs_end))
    rsd1s, rsd1e = (halves(step, 1) for step in (rsd_start, rsd_end))

    def when(condition, *steps):
        def run():
            for step, c in steps:
                step(c)

        pl.when(condition)(run)

    make_pieces(0)
    pl.semaphore_wait(barrier, len(partners))
    quad_send(0)
    for c in range(1, CH):
        make_pieces(c)
        quad_send(c)
    exchange(0, core).start()
    loads[0].wait()
    quad_done(0)
    agd0s(0)
    transpose_rows(core * 2)
    for k in (1, 2):
        exchange(k, core).start()
    quad_done(1)
    agd0s(1)
    agd0e(0)
    ag1s(0)
    quad_done(2)
    agd0s(2)
    transpose_rows(core * 2 + 1)
    agd0e(1)
    ag1s(1)
    quad_done(3)
    agd0s(3)
    ag1m(0)
    for k in range(BLOCKS):
        strips[1][k].wait()
    for k in range(2):
        peer_copy(k).start()
    exchange(0, other).wait_recv()
    transpose_rows(other * 2)
    agd0e(2)
    ag1s(2)
    transpose_rows(other * 2 + 1)
    for k in (1, 2):
        exchange(k, other).wait_recv()
    for k in (1, 2, 3, 4):
        loads[k].wait()

    def work(c):
        ag1e(c)

        project(c)
        when(c == 0, (ag1m, 1))
        when(c > 1, (rsd1e, c - 2), (z_send, c - 2))

        def pair(i, _):
            attend(c, 2 * i)
            attend(c, 2 * i + 1)
            when((c == 0) & (i == 0), (agd0e, 3), (ag1s, 3))
            when((c == 1) & (i == 0), (ag1m, 3))
            when((c > 0) & (i == 0), (rs0m, c - 1))
            when((c > 1) & (i == 1), (z_done, c - 2))
            return 0

        def part(i, _):
            gradient(c, i)
            when((c == 0) & (i == 0), (ag1m, 2))
            when((c > 0) & (i == 0), (rs0e, c - 1), (rsd1s, c - 1))
            return 0

        lax.fori_loop(0, 2, pair, 0)
        lax.fori_loop(0, 2, part, 0)
        rs0s(c)

    each(work)
    last = CH - 1
    rsd1e(last - 1)
    z_send(last - 1)
    for k in range(2):
        peer_copy(k).wait_recv()
    finish(0)
    rs0m(last)
    z_done(last - 1)
    finish(1)
    rs0e(last)
    rsd1s(last)
    finish(last - 1)
    rsd1e(last)
    z_send(last)
    z_done(last)
    finish(last)

    def drain(c):
        for k, (where, _, d) in enumerate(quad):
            rc(b["piece"].at[c, d], b["pin"].at[c, my_slot], c, M_QUAD + k, where).wait_send()
        for half in range(2):
            for phase in range(2):
                me = axis_of(half, phase)["me"]
                if phase == 0:
                    for k in range(3):
                        agd_copy(c, half, phase, k, me).wait_send()
                    for k in range(6):
                        rs_copy(c, half, phase, k).wait_send()
                else:
                    for k in range(4):
                        ag_copy(c, half, phase, k, up(me, (0, 0, 3, 1)[k])).wait_send()
                    for k in range(3):
                        for part in ("p", "q"):
                            rsd_copy(c, half, phase, k, part).wait_send()
        z_copy(c).wait_send()
        fix_copy(c, core).wait_send()
        for rel in (0, 1):
            gossip_copy(c, rel, core).wait_send()

    each(drain)
    for k in range(3):
        exchange(k, core).wait_send()
    for i in range(2):
        for k in range(BLOCKS):
            out_copy(i, k).wait()
    for k in range(2):
        peer_copy(k).wait_send()


def step_kernel(distance):
    anywhere = pl.BlockSpec(memory_space=pl.ANY)
    return pl.pallas_call(
        functools.partial(kernel, distance),
        out_shape=[jax.ShapeDtypeStruct((OWN, BLOCKS, 128), F32)] * 2,
        in_specs=[pl.BlockSpec(memory_space=pltpu.SMEM)] + [anywhere] * 7,
        out_specs=[anywhere, anywhere],
        scratch_shapes=[pltpu.VMEM(shape, dtype) for shape, dtype in SCRATCH.values()]
        + [
            pltpu.SemaphoreType.DMA((CH, M_ALL)),
            pltpu.SemaphoreType.DMA((CH, M_ALL)),
            pltpu.SemaphoreType.DMA((5,)),
            pltpu.SemaphoreType.DMA((5,)),
            pltpu.SemaphoreType.DMA((5,)),
            pltpu.SemaphoreType.DMA((2, BLOCKS)),
            pltpu.SemaphoreType.DMA((2, BLOCKS)),
        ],
        compiler_params=pltpu.CompilerParams(
            collective_id=distance, has_side_effects=True, vmem_limit_bytes=60 * 2**20),
        cost_estimate=pl.CostEstimate(flops=13 * 10**9, bytes_accessed=10**7, transcendentals=4 * 10**6),
    )


def shards(step_index, tokens, queries, cotangent, params, momentum):
    cos, sin = rope_tables()
    operands = (step_index, tokens, queries, cotangent, params.reshape(OWN, BLOCKS, 128),
                momentum.reshape(OWN, BLOCKS, 128), jnp.asarray(cos), jnp.asarray(sin))
    sum_p, sum_m = lax.cond(
        (step_index[0] & 1) == 0, *[lambda *xs, d=d: tuple(step_kernel(d)(*xs)) for d in (1, 2)], *operands)
    return (0.5 * sum_p).reshape(1, OWN, WIDE), (0.5 * sum_m).reshape(1, OWN, WIDE)


def solution(mesh):
    rows = P("rep", "fsdp", None)
    return jax.shard_map(
        shards,
        mesh=mesh,
        in_specs=(P(), rows, rows, rows, rows, rows),
        out_specs=(rows, rows),
        check_vma=False,
    )
```

```python
import functools

import jax
import jax.numpy as jnp
import numpy as np
from jax import lax
from jax.experimental import pallas as pl
from jax.experimental.pallas import tpu as pltpu
from jax.sharding import PartitionSpec as P

MESH = pl.DeviceIdType.MESH
F32 = jnp.float32
BF16 = jnp.bfloat16

HEAD = 128
LENGTH = 256
SOFT_CAP = 50.0
SCORE_SCALE = 144.0 ** (-0.5)
ROPE_THETA = 10000.0
LEARN_RATE = 0.1
WARM_SPAN = 64.0
MOMENTUM_DECAY = 0.9
LOG2E = 1.4426950408889634

D = 2304
TOK = 512
CH = 4
ROWS = 144
OWN = 36
WIDE = 2048
BLOCKS = WIDE // 128

M_QUAD = 0
M_AG = 3
M_RS = 19
M_Z = 43
M_FIX = 44
M_GOS = 45
M_ALL = 47


def rope_tables():
    half = HEAD // 2
    inverse = np.float32(ROPE_THETA) ** (-np.arange(half, dtype=np.float32) / np.float32(half))
    angles = np.arange(LENGTH, dtype=np.float32)[:, None] * inverse[None, :].astype(np.float32)
    cos, sin = np.cos(angles), np.sin(angles)
    cos_full = np.concatenate([cos, cos], axis=1).astype(np.float32)
    sin_signed = np.concatenate([-sin, sin], axis=1).astype(np.float32)
    return cos_full, sin_signed


def m16(value, by=16):
    return pl.multiple_of(value, by)


SCRATCH = dict(
    tok=((2 * TOK, D), BF16),
    tok_t=((D, 2 * TOK), BF16),
    q=((2 * TOK, 1024), BF16),
    cot=((2 * TOK, 1024), BF16),
    p=((BLOCKS, OWN, 128), F32),
    m=((BLOCKS, OWN, 128), F32),
    peer=((2, BLOCKS, OWN, 128), F32),
    out_p=((BLOCKS, OWN, 128), F32),
    out_m=((BLOCKS, OWN, 128), F32),
    cos=((LENGTH, HEAD), F32),
    sin=((LENGTH, HEAD), F32),
    piece=((CH, 2, 80, 128), BF16),
    pin=((CH, 4, 80, 128), BF16),
    w=((CH, 4, 576, 256), BF16),
    joined=((2 * TOK, 256), BF16),
    grads=((2 * TOK, 256), BF16),
    f=((CH, 4, 576, 256), F32),
    g=((CH, 4, 576, 256), BF16),
    h=((CH, 2, 4, ROWS, 128), F32),
    hb=((CH, 2, 4, ROWS, 128), BF16),
    e=((CH, ROWS, 256), F32),
    zs=((CH, 80, 256), BF16),
    zr=((CH, 80, 256), BF16),
    fs=((CH, 72, 128), F32),
    gx=((CH, 2, 72, 128), F32),
    gb=((CH, 2, 80, 128), BF16),
    gp=((CH, 2, 80, 128), BF16),
)
PARTS = ("al", "bl", "cl", "ar", "br", "cr", "tr", "tl")
P_PARTS = ("al", "cl", "br", "tr")
for _name in PARTS:
    SCRATCH["x0" + _name] = ((CH, 2, ROWS, 128), BF16)
    SCRATCH["x1" + _name] = ((CH, 288, 128), BF16)
    for _half in (0, 1):
        SCRATCH["y%d%s" % (_half, _name)] = ((CH, 80 if _name in P_PARTS else 64, 128), BF16)
NAMES = tuple(SCRATCH)


def kernel(distance, step_ref, tok_h, q_h, cot_h, p_h, m_h, cos_h, sin_h, outp_h, outm_h, *scratch):
    b = dict(zip(NAMES, scratch))
    ssem, rsem, gssem, grsem, lsem, psem, osem = scratch[len(NAMES):]
    rep = lax.axis_index("rep")
    f = lax.axis_index("fsdp")
    core = lax.rem(f, 2)
    zh = lax.rem(f // 2, 2)
    x = lax.rem(f // 4, 4)
    y = f // 16
    other = 1 - core

    def dev(r=rep, yy=y, xx=x, zz=zh, cc=core):
        return (r, ((yy * 4 + xx) * 2 + zz) * 2 + cc)

    def up(i, by=1):
        return lax.rem(i + by, 4)

    side = {
        "x": dict(me=x, r=dev(xx=up(x)), l=dev(xx=up(x, 3))),
        "y": dict(me=y, r=dev(yy=up(y)), l=dev(yy=up(y, 3))),
    }

    def axis_of(half, phase):
        return side["x" if half == phase else "y"]

    def axis_rs(half, phase):
        return side["x" if half == phase else "y"]

    def rc(src, dst, c, k, where):
        return pltpu.make_async_remote_copy(
            src_ref=src, dst_ref=dst, send_sem=ssem.at[c, k], recv_sem=rsem.at[c, k],
            device_id=where, device_id_type=MESH)

    my_rows = pl.ds(m16(core * TOK, TOK), TOK)
    my_cols = pl.ds(m16(core * 1024, 1024), 1024)
    other_cols = pl.ds(m16(other * 1024, 1024), 1024)
    loads = [
        pltpu.make_async_copy(tok_h.at[0], b["tok"].at[my_rows, :], lsem.at[2]),
        pltpu.make_async_copy(q_h.at[0, :, my_cols], b["q"].at[my_rows, :], lsem.at[3]),
        pltpu.make_async_copy(cot_h.at[0, :, my_cols], b["cot"].at[my_rows, :], lsem.at[4]),
    ]
    loads += [
        pltpu.make_async_copy(cos_h, b["cos"], lsem.at[0]),
        pltpu.make_async_copy(sin_h, b["sin"], lsem.at[1]),
    ]
    strips = [[pltpu.make_async_copy(ref.at[:, k, :], b["pm"[i]].at[k], psem.at[i, k]) for k in range(BLOCKS)]
              for i, ref in enumerate((p_h, m_h))]
    order = [kd + c for c in range(CH) for kd in (0, 4, 8, 12)]
    for k in order:
        strips[0][k].start()
    for load in loads:
        load.start()
    for k in order:
        strips[1][k].start()

    barrier = pltpu.get_barrier_semaphore()
    partners = [dev(cc=other), dev(zz=1 - zh), dev(zz=1 - zh, cc=other)]
    partners += [side[a][d] for a in ("x", "y") for d in ("r", "l")]
    partners += [dev(xx=up(x, 2)), dev(yy=up(y, 2))]
    partners += [dev(r=up(rep, d), cc=cc) for d in sorted({distance, 4 - distance}) for cc in (core, other)]
    for partner in partners:
        pl.semaphore_signal(barrier, inc=1, device_id=partner, device_id_type=MESH)

    def make_pieces(c):
        for kd in (0, 4, 8, 12):
            strips[0][kd + c].wait()
        for d in range(2):
            v = [b["p"][d * 4 + c], b["p"][8 + d * 4 + c], jnp.zeros((8, 128), F32)]
            b["piece"][c, d] = jnp.concatenate(v, axis=0).astype(BF16)

    quad = [(dev(cc=other), zh * 2 + other, other),
            (dev(zz=1 - zh), (1 - zh) * 2 + core, core),
            (dev(zz=1 - zh, cc=other), (1 - zh) * 2 + other, other)]
    my_slot = zh * 2 + core

    def quad_send(c):
        for k, (where, _, d) in enumerate(quad):
            rc(b["piece"].at[c, d], b["pin"].at[c, my_slot], c, M_QUAD + k, where).start()

    def quad_done(c):
        for k, (where, slot, d) in enumerate(quad):
            rc(b["piece"].at[c, d], b["pin"].at[c, slot], c, M_QUAD + k, where).wait_recv()
        b["pin"][c, my_slot] = b["piece"][c, core]
        v = [b["pin"][c, s].astype(F32) for s in range(4)]
        for kv in range(2):
            block = jnp.concatenate([u[kv * OWN:(kv + 1) * OWN] for u in v], axis=0)
            b["w"][c, y, pl.ds(m16(x * ROWS), ROWS), pl.ds(kv * 128, 128)] = block.astype(BF16)

    def w_unit(c, half, phase, j, part):
        lanes = pl.ds(half * 128, 128)
        w = b["w"]
        if phase == 0:
            at, n = dict(all=(0, ROWS), p=(0, 80), q=(80, 64))[part]
            if half == 0:
                return w.at[c, y, pl.ds(m16(j * ROWS + at), n), lanes]
            return w.at[c, j, pl.ds(m16(x * ROWS + at), n), lanes]
        if half == 0:
            at, n = dict(all=(0, 576), p=(0, 288), q=(288, 288))[part]
            return w.at[c, j, pl.ds(at, n), lanes]
        at, n = dict(all=(0, 4), p=(0, 2), q=(2, 2))[part]
        return w.at[c, pl.ds(at, n), pl.ds(m16(j * ROWS), ROWS), lanes]

    def far(half, phase):
        return dev(xx=up(x, 2)) if half == phase else dev(yy=up(y, 2))

    def ag_copy(c, half, phase, k, j):
        s = axis_of(half, phase)
        unit = w_unit(c, half, phase, j, ("all", "all", "p", "q")[k])
        return rc(unit, unit, c, M_AG + half * 8 + phase * 4 + k, s["r"] if k % 2 == 0 else s["l"])

    def ag_start(c, half, phase):
        me = axis_of(half, phase)["me"]
        ag_copy(c, half, phase, 0, me).start()
        ag_copy(c, half, phase, 1, me).start()

    def ag_mid(c, half, phase):
        me = axis_of(half, phase)["me"]
        ag_copy(c, half, phase, 0, up(me, 3)).wait_recv()
        ag_copy(c, half, phase, 2, up(me, 3)).start()
        ag_copy(c, half, phase, 1, up(me)).wait_recv()
        ag_copy(c, half, phase, 3, up(me)).start()

    def ag_end(c, half, phase):
        me = axis_of(half, phase)["me"]
        ag_copy(c, half, phase, 2, up(me, 2)).wait_recv()
        ag_copy(c, half, phase, 3, up(me, 2)).wait_recv()

    def transpose_rows(s):
        rows = pl.ds(m16(s * 256, 256), 256)

        def one(k, _):
            cols = pl.ds(m16(k * 256, 256), 256)
            b["tok_t"][cols, rows] = b["tok"][rows, cols].T
            return 0

        lax.fori_loop(0, D // 256, one, 0)

    half_len = LENGTH // 2
    triangle = lax.broadcasted_iota(jnp.int32, (half_len, LENGTH), 0) <= lax.rem(
        lax.broadcasted_iota(jnp.int32, (half_len, LENGTH), 1), half_len)
    scale_in = D ** (-0.5)

    def nt(a, bb):
        return lax.dot_general(a, bb, (((1,), (1,)), ((), ())), preferred_element_type=F32)

    def project(c):
        w = b["w"][c].reshape(D, 256)
        b["joined"][...] = (jnp.dot(b["tok"][...], w, preferred_element_type=F32) * scale_in).astype(BF16)

    def attend(c, s):
        rows = pl.ds(m16(s * 256, 256), 256)
        joined = b["joined"][rows, :]
        key = joined[:, :HEAD].astype(F32)
        val = joined[:, HEAD:]
        cos, sin = b["cos"][...], b["sin"][...]
        rot = (key * cos + pltpu.roll(key, 64, 1) * sin).astype(BF16)
        d_val, d_rot = [], []
        for block in range(2):
            at = pl.ds(m16(s * LENGTH + block * half_len, half_len), half_len)
            cols = [pl.ds(m16(c * 256 + head * 128, 128), 128) for head in range(2)]
            qh = jnp.concatenate([b["q"][at, col] for col in cols], axis=0)
            ch = jnp.concatenate([b["cot"][at, col] for col in cols], axis=0)
            keys = half_len * (block + 1)
            bent = jnp.tanh(nt(rot[:keys], qh) * (SCORE_SCALE / SOFT_CAP))
            weights = jnp.exp2(bent * (SOFT_CAP * LOG2E))
            masked = jnp.where(triangle, weights[keys - half_len:], 0.0)
            weights = masked if block == 0 else jnp.concatenate([weights[:half_len], masked], axis=0)
            shares = weights * (1.0 / jnp.sum(weights, axis=0, keepdims=True))
            d_val.append(jnp.dot(shares.astype(BF16), ch, preferred_element_type=F32))
            share_grad = nt(val[:keys], ch)
            mean = jnp.sum(shares * share_grad, axis=0, keepdims=True)
            score = shares * (share_grad - mean) * (SCORE_SCALE - bent * bent * SCORE_SCALE)
            d_rot.append(jnp.dot(score.astype(BF16), qh, preferred_element_type=F32))
        d_val, d_rot = (jnp.concatenate([hi[:half_len] + lo, hi[half_len:]], axis=0) for lo, hi in (d_val, d_rot))
        d_key = d_rot * cos - pltpu.roll(d_rot, 64, 1) * sin
        b["grads"][rows, :] = (jnp.concatenate([d_key, d_val], axis=1) * scale_in).astype(BF16)

    def gradient(c, part):
        rows = pl.ds(m16(part * 1152, 128), 1152)
        v = jnp.dot(b["tok_t"][rows, :], b["grads"][...], preferred_element_type=F32).reshape(2, 576, 256)
        at = pl.ds(part * 2, 2)
        b["f"][c, at] = v
        b["g"][c, at] = v.astype(BF16)

    def unit(name, c, half, phase, j, part):
        if phase == 0:
            ref = b["f" if name == "f" else "g"]
            if half == 0:
                return ref.at[c, pl.ds(0 if part == "p" else 2, 2), pl.ds(m16(j * ROWS), ROWS), pl.ds(0, 128)]
            return ref.at[c, j, pl.ds(0 if part == "p" else 288, 288), pl.ds(128, 128)]
        ref = b["h" if name == "f" else "hb"]
        return ref.at[c, half, j, pl.ds(0, 80) if part == "p" else pl.ds(80, 64), :]

    def buf(c, half, phase, name):
        return b["xy"[phase] + str(half) + name].at[c]

    RS_DST = ("al", "ar", "bl", "br", "cl", "cr")
    RS_PART = ("p", "q", "q", "p", "p", "q")

    def rs_copy(c, half, phase, k):
        s = axis_rs(half, phase)
        me = s["me"]
        if k < 4:
            j = (up(me, 2), up(me, 2), up(me), up(me, 3))[k]
            src = unit("g", c, half, phase, j, RS_PART[k])
        else:
            src = buf(c, half, phase, "tr" if k == 4 else "tl")
        return rc(src, buf(c, half, phase, RS_DST[k]), c, M_RS + half * 12 + phase * 6 + k,
                  s["r"] if k % 2 == 0 else s["l"])

    def rs_start(c, half, phase):
        for k in range(4):
            rs_copy(c, half, phase, k).start()

    def rs_mid(c, half, phase):
        me = axis_rs(half, phase)["me"]
        for k, j, part, arrived, out in ((0, up(me), "p", "al", "tr"), (1, up(me, 3), "q", "ar", "tl")):
            rs_copy(c, half, phase, k).wait_recv()
            total = unit("f", c, half, phase, j, part)[...] + buf(c, half, phase, arrived)[...].astype(F32)
            buf(c, half, phase, out)[...] = total.astype(BF16)
            rs_copy(c, half, phase, 4 + k).start()

    def rs_end(c, half, phase):
        me = axis_rs(half, phase)["me"]
        for k in range(2, 6):
            rs_copy(c, half, phase, k).wait_recv()
        for part, one, two in (("p", "cl", "br"), ("q", "bl", "cr")):
            total = (unit("f", c, half, phase, me, part)[...]
                     + buf(c, half, phase, one)[...].astype(F32) + buf(c, half, phase, two)[...].astype(F32))
            if phase == 0:
                at = pl.ds(0 if part == "p" else 2, 2)
                total = total.reshape(2, ROWS, 128)
                b["h"][c, half, at] = total
                b["hb"][c, half, at] = total.astype(BF16)
            else:
                at = pl.ds(0, 80) if part == "p" else pl.ds(80, 64)
                b["e"][c, at, pl.ds(half * 128, 128)] = total

    def z_copy(c):
        return rc(b["zs"].at[c], b["zr"].at[c], c, M_Z, dev(zz=1 - zh))

    def z_send(c):
        v = b["e"][c]
        b["zs"][c] = jnp.where(zh == 0, v[64:], v[:80]).astype(BF16)
        z_copy(c).start()

    def fix_copy(c, slot):
        return rc(b["fs"].at[c], b["gx"].at[c, slot], c, M_FIX, dev(cc=other))

    def gossip_copy(c, rel, slot):
        to = core if rel == 0 else other
        return rc(b["gb"].at[c, to], b["gp"].at[c, slot], c, M_GOS + rel,
                  dev(r=up(rep, distance), cc=to))

    def z_done(c):
        z_copy(c).wait_recv()
        v = b["e"][c]
        r = b["zr"][c].astype(F32)
        total = jnp.where(zh == 0, v[:72], v[72:]) + jnp.where(zh == 0, r[:72], r[8:])
        first, last = (jnp.concatenate([total[r:r + OWN, :128], total[r:r + OWN, 128:]], axis=0) for r in (0, OWN))
        pad = jnp.zeros((8, 128), F32)
        b["gb"][c, 0] = jnp.concatenate([first, pad], axis=0).astype(BF16)
        b["gb"][c, 1] = jnp.concatenate([last, pad], axis=0).astype(BF16)
        b["fs"][c] = jnp.where(core == 0, last, first)
        b["gx"][c, core] = jnp.where(core == 0, first, last)
        for rel in (0, 1):
            gossip_copy(c, rel, core).start()
        fix_copy(c, core).start()

    t = step_ref[0]
    learn_now = LEARN_RATE * (t.astype(F32) + 1.0) / WARM_SPAN

    def out_copy(i, k):
        return pltpu.make_async_copy(b[("out_p", "out_m")[i]].at[k], (outp_h, outm_h)[i].at[:, k, :], osem.at[i, k])

    def finish(c):
        fix_copy(c, other).wait_recv()
        for rel in (0, 1):
            gossip_copy(c, rel, core if rel == 0 else other).wait_recv()
        for d in range(2):
            own = b["gx"][c, d]
            peer = b["gp"][c, d].astype(F32)
            for kv in range(2):
                at = kv * 8 + d * 4 + c
                mom = MOMENTUM_DECAY * b["m"][at] + own[kv * OWN:(kv + 1) * OWN]
                mom2 = MOMENTUM_DECAY * b["peer"][1, at] + peer[kv * OWN:(kv + 1) * OWN]
                b["out_m"][at] = mom + mom2
                b["out_p"][at] = (b["p"][at] - learn_now * mom) + (b["peer"][0, at] - learn_now * mom2)
                for i in range(2):
                    out_copy(i, at).start()

    def exchange(k, slot):
        src = (tok_h.at[0], q_h.at[0, :, other_cols], cot_h.at[0, :, other_cols])[k]
        dst = b[("tok", "q", "cot")[k]].at[pl.ds(m16(slot * TOK, TOK), TOK), :]
        return pltpu.make_async_remote_copy(
            src_ref=src, dst_ref=dst, send_sem=gssem.at[k], recv_sem=grsem.at[k],
            device_id=dev(cc=other), device_id_type=MESH)

    def peer_copy(k):
        at = 3 + k
        return pltpu.make_async_remote_copy(
            src_ref=b["pm"[k]], dst_ref=b["peer"].at[k], send_sem=gssem.at[at],
            recv_sem=grsem.at[at], device_id=dev(r=up(rep, distance)), device_id_type=MESH)

    def each(*steps):
        def body(c, _):
            for step in steps:
                step(c)
            return 0

        lax.fori_loop(0, CH, body, 0)

    def halves(step, phase):
        def run(c):
            step(c, 0, phase)
            step(c, 1, phase)

        return run

    def agd_copy(c, half, phase, k, j):
        s = axis_of(half, phase)
        block = w_unit(c, half, phase, j, "all")
        return rc(block, block, c, M_AG + half * 8 + phase * 4 + k, (s["r"], s["l"], far(half, phase))[k])

    def agd_start(c, half, phase):
        me = axis_of(half, phase)["me"]
        for k in (2, 0, 1):
            agd_copy(c, half, phase, k, me).start()

    def agd_end(c, half, phase):
        me = axis_of(half, phase)["me"]
        for k, by in ((0, 3), (1, 1), (2, 2)):
            agd_copy(c, half, phase, k, up(me, by)).wait_recv()

    def rsd_copy(c, half, phase, k, part):
        s = axis_rs(half, phase)
        me = s["me"]
        j = (up(me), up(me, 3), up(me, 2))[k]
        src = unit("g", c, half, phase, j, part)
        name = {"p": ("al", "br", "cl"), "q": ("ar", "bl", "cr")}[part][k]
        return rc(src, buf(c, half, phase, name), c, M_RS + half * 12 + phase * 6 + k * 2 + (part == "q"),
                  (s["r"], s["l"], far(half, phase))[k])

    def rsd_start(c, half, phase):
        for k in (2, 0, 1):
            for part in ("p", "q"):
                rsd_copy(c, half, phase, k, part).start()

    def rsd_end(c, half, phase):
        me = axis_rs(half, phase)["me"]
        for part in ("p", "q"):
            for k in range(3):
                rsd_copy(c, half, phase, k, part).wait_recv()
        for part, names in (("p", ("al", "br", "cl")), ("q", ("ar", "bl", "cr"))):
            total = unit("f", c, half, phase, me, part)[...]
            for name in names:
                total += buf(c, half, phase, name)[...].astype(F32)
            if phase == 0:
                at = pl.ds(0 if part == "p" else 2, 2)
                total = total.reshape(2, ROWS, 128)
                b["h"][c, half, at] = total
                b["hb"][c, half, at] = total.astype(BF16)
            else:
                at = pl.ds(0, 80) if part == "p" else pl.ds(80, 64)
                b["e"][c, at, pl.ds(half * 128, 128)] = total

    agd0s, agd0e = (halves(step, 0) for step in (agd_start, agd_end))
    ag1s, ag1m, ag1e = (halves(step, 1) for step in (ag_start, ag_mid, ag_end))
    rs0s, rs0m, rs0e = (halves(step, 0) for step in (rs_start, rs_mid, rs_end))
    rsd1s, rsd1e = (halves(step, 1) for step in (rsd_start, rsd_end))

    def when(condition, *steps):
        def run():
            for step, c in steps:
                step(c)

        pl.when(condition)(run)

    make_pieces(0)
    pl.semaphore_wait(barrier, len(partners))
    quad_send(0)
    for c in range(1, CH):
        make_pieces(c)
        quad_send(c)
    exchange(0, core).start()
    loads[0].wait()
    quad_done(0)
    agd0s(0)
    transpose_rows(core * 2)
    for k in (1, 2):
        exchange(k, core).start()
    quad_done(1)
    agd0s(1)
    agd0e(0)
    ag1s(0)
    quad_done(2)
    agd0s(2)
    transpose_rows(core * 2 + 1)
    agd0e(1)
    ag1s(1)
    quad_done(3)
    agd0s(3)
    ag1m(0)
    for k in range(BLOCKS):
        strips[1][k].wait()
    for k in range(2):
        peer_copy(k).start()
    exchange(0, other).wait_recv()
    transpose_rows(other * 2)
    agd0e(2)
    ag1s(2)
    ag1m(1)
    agd0e(3)
    ag1s(3)
    transpose_rows(other * 2 + 1)
    for k in (1, 2):
        exchange(k, other).wait_recv()
    for k in (1, 2, 3, 4):
        loads[k].wait()

    def work(c):
        ag1e(c)

        project(c)
        when(c == 1, (ag1m, 3))
        when(c > 1, (rs0e, c - 2), (rsd1s, c - 2))

        def pair(i, _):
            attend(c, 2 * i)
            attend(c, 2 * i + 1)
            when((c == 0) & (i == 0), (ag1m, 2))
            when((c == CH - 1) & (i == 0), (z_done, 0))
            when((c > 0) & (i == 1), (rs0m, c - 1))
            return 0

        def part(i, _):
            gradient(c, i)
            when((c > 1) & (i == 0), (rsd1e, c - 2), (z_send, c - 2))
            return 0

        lax.fori_loop(0, 2, pair, 0)
        lax.fori_loop(0, 2, part, 0)
        rs0s(c)

    def drain_gather(c):
        for k, (where, _, d) in enumerate(quad):
            rc(b["piece"].at[c, d], b["pin"].at[c, my_slot], c, M_QUAD + k, where).wait_send()
        for half in range(2):
            me = axis_of(half, 0)["me"]
            for k in range(3):
                agd_copy(c, half, 0, k, me).wait_send()
            me = axis_of(half, 1)["me"]
            for k in range(4):
                ag_copy(c, half, 1, k, up(me, (0, 0, 3, 1)[k])).wait_send()

    def drain_wide(c):
        for half in range(2):
            for k in range(6):
                rs_copy(c, half, 0, k).wait_send()

    def drain_narrow(c):
        for half in range(2):
            for k in range(3):
                for part in ("p", "q"):
                    rsd_copy(c, half, 1, k, part).wait_send()

    def drain_end(c):
        z_copy(c).wait_send()
        fix_copy(c, core).wait_send()
        for rel in (0, 1):
            gossip_copy(c, rel, core).wait_send()
        for i in range(2):
            for k in (0, 4, 8, 12):
                out_copy(i, k + c).wait()

    each(work)
    last = CH - 1
    each(drain_gather)
    rs0e(last - 1)
    rsd1s(last - 1)
    rs0m(last)
    z_done(last - 2)
    drain_wide(0)
    rsd1e(last - 1)
    z_send(last - 1)
    for k in range(2):
        peer_copy(k).wait_recv()
    finish(0)
    rs0e(last)
    rsd1s(last)
    finish(1)
    drain_wide(1)
    drain_wide(2)
    z_done(last - 1)
    drain_narrow(0)
    drain_narrow(1)
    rsd1e(last)
    z_send(last)
    finish(last - 1)
    drain_wide(3)
    drain_narrow(2)
    for k in range(3):
        exchange(k, core).wait_send()
    for k in range(2):
        peer_copy(k).wait_send()
    z_done(last)
    drain_narrow(3)
    for c in range(last):
        drain_end(c)
    finish(last)
    drain_end(last)


def step_kernel(distance):
    anywhere = pl.BlockSpec(memory_space=pl.ANY)
    return pl.pallas_call(
        functools.partial(kernel, distance),
        out_shape=[jax.ShapeDtypeStruct((OWN, BLOCKS, 128), F32)] * 2,
        in_specs=[pl.BlockSpec(memory_space=pltpu.SMEM)] + [anywhere] * 7,
        out_specs=[anywhere, anywhere],
        scratch_shapes=[pltpu.VMEM(shape, dtype) for shape, dtype in SCRATCH.values()]
        + [
            pltpu.SemaphoreType.DMA((CH, M_ALL)),
            pltpu.SemaphoreType.DMA((CH, M_ALL)),
            pltpu.SemaphoreType.DMA((5,)),
            pltpu.SemaphoreType.DMA((5,)),
            pltpu.SemaphoreType.DMA((5,)),
            pltpu.SemaphoreType.DMA((2, BLOCKS)),
            pltpu.SemaphoreType.DMA((2, BLOCKS)),
        ],
        compiler_params=pltpu.CompilerParams(
            collective_id=distance, has_side_effects=True, vmem_limit_bytes=60 * 2**20),
        cost_estimate=pl.CostEstimate(flops=13 * 10**9, bytes_accessed=10**7, transcendentals=4 * 10**6),
    )


def shards(step_index, tokens, queries, cotangent, params, momentum):
    cos, sin = rope_tables()
    operands = (step_index, tokens, queries, cotangent, params.reshape(OWN, BLOCKS, 128),
                momentum.reshape(OWN, BLOCKS, 128), jnp.asarray(cos), jnp.asarray(sin))
    sum_p, sum_m = lax.cond(
        (step_index[0] & 1) == 0, *[lambda *xs, d=d: tuple(step_kernel(d)(*xs)) for d in (1, 2)], *operands)
    return (0.5 * sum_p).reshape(1, OWN, WIDE), (0.5 * sum_m).reshape(1, OWN, WIDE)


def solution(mesh):
    rows = P("rep", "fsdp", None)
    return jax.shard_map(
        shards,
        mesh=mesh,
        in_specs=(P(), rows, rows, rows, rows, rows),
        out_specs=(rows, rows),
        check_vma=False,
    )
```

```python
import functools

import jax
import jax.numpy as jnp
import numpy as np
from jax import lax
from jax.experimental import pallas as pl
from jax.experimental.pallas import tpu as pltpu
from jax.sharding import PartitionSpec as P

MESH = pl.DeviceIdType.MESH
F32 = jnp.float32
BF16 = jnp.bfloat16

HEAD = 128
LENGTH = 256
SOFT_CAP = 50.0
SCORE_SCALE = 144.0 ** (-0.5)
ROPE_THETA = 10000.0
LEARN_RATE = 0.1
WARM_SPAN = 64.0
MOMENTUM_DECAY = 0.9
LOG2E = 1.4426950408889634

D = 2304
TOK = 512
CH = 4
ROWS = 144
OWN = 36
WIDE = 2048
BLOCKS = WIDE // 128

M_QUAD = 0
M_AG = 3
M_RS = 19
M_Z = 43
M_FIX = 44
M_GOS = 45
M_ALL = 47


def rope_tables():
    half = HEAD // 2
    inverse = np.float32(ROPE_THETA) ** (-np.arange(half, dtype=np.float32) / np.float32(half))
    angles = np.arange(LENGTH, dtype=np.float32)[:, None] * inverse[None, :].astype(np.float32)
    cos, sin = np.cos(angles), np.sin(angles)
    cos_full = np.concatenate([cos, cos], axis=1).astype(np.float32)
    sin_signed = np.concatenate([-sin, sin], axis=1).astype(np.float32)
    return cos_full, sin_signed


def m16(value, by=16):
    return pl.multiple_of(value, by)


SCRATCH = dict(
    tok=((2 * TOK, D), BF16),
    tok_t=((D, 2 * TOK), BF16),
    q=((2 * TOK, 1024), BF16),
    cot=((2 * TOK, 1024), BF16),
    p=((BLOCKS, OWN, 128), F32),
    m=((BLOCKS, OWN, 128), F32),
    peer=((2, BLOCKS, OWN, 128), F32),
    out_p=((BLOCKS, OWN, 128), F32),
    out_m=((BLOCKS, OWN, 128), F32),
    cos=((LENGTH, HEAD), F32),
    sin=((LENGTH, HEAD), F32),
    piece=((CH, 2, 80, 128), BF16),
    pin=((CH, 4, 80, 128), BF16),
    w=((CH, 4, 576, 256), BF16),
    joined=((2 * TOK, 256), BF16),
    grads=((2 * TOK, 256), BF16),
    f=((CH, 4, 576, 256), F32),
    g=((CH, 4, 576, 256), BF16),
    h=((CH, 2, 4, ROWS, 128), F32),
    hb=((CH, 2, 4, ROWS, 128), BF16),
    e=((CH, ROWS, 256), F32),
    zs=((CH, 80, 256), BF16),
    zr=((CH, 80, 256), BF16),
    fs=((CH, 72, 128), F32),
    gx=((CH, 2, 72, 128), F32),
    gb=((CH, 2, 80, 128), BF16),
    gp=((CH, 2, 80, 128), BF16),
)
PARTS = ("al", "bl", "cl", "ar", "br", "cr", "tr", "tl")
P_PARTS = ("al", "cl", "br", "tr")
for _name in PARTS:
    SCRATCH["x0" + _name] = ((CH, 2, ROWS, 128), BF16)
    SCRATCH["x1" + _name] = ((CH, 288, 128), BF16)
    for _half in (0, 1):
        SCRATCH["y%d%s" % (_half, _name)] = ((CH, 80 if _name in P_PARTS else 64, 128), BF16)
NAMES = tuple(SCRATCH)


def kernel(distance, step_ref, tok_h, q_h, cot_h, p_h, m_h, cos_h, sin_h, outp_h, outm_h, *scratch):
    b = dict(zip(NAMES, scratch))
    ssem, rsem, gssem, grsem, lsem, psem, osem = scratch[len(NAMES):]
    rep = lax.axis_index("rep")
    f = lax.axis_index("fsdp")
    core = lax.rem(f, 2)
    zh = lax.rem(f // 2, 2)
    x = lax.rem(f // 4, 4)
    y = f // 16
    other = 1 - core

    def dev(r=rep, yy=y, xx=x, zz=zh, cc=core):
        return (r, ((yy * 4 + xx) * 2 + zz) * 2 + cc)

    def up(i, by=1):
        return lax.rem(i + by, 4)

    side = {
        "x": dict(me=x, r=dev(xx=up(x)), l=dev(xx=up(x, 3))),
        "y": dict(me=y, r=dev(yy=up(y)), l=dev(yy=up(y, 3))),
    }

    def axis_of(half, phase):
        return side["x" if half == phase else "y"]

    def axis_rs(half, phase):
        return side["x" if half == phase else "y"]

    def rc(src, dst, c, k, where):
        return pltpu.make_async_remote_copy(
            src_ref=src, dst_ref=dst, send_sem=ssem.at[c, k], recv_sem=rsem.at[c, k],
            device_id=where, device_id_type=MESH)

    my_rows = pl.ds(m16(core * TOK, TOK), TOK)
    my_cols = pl.ds(m16(core * 1024, 1024), 1024)
    other_cols = pl.ds(m16(other * 1024, 1024), 1024)
    loads = [
        pltpu.make_async_copy(tok_h.at[0], b["tok"].at[my_rows, :], lsem.at[2]),
        pltpu.make_async_copy(q_h.at[0, :, my_cols], b["q"].at[my_rows, :], lsem.at[3]),
        pltpu.make_async_copy(cot_h.at[0, :, my_cols], b["cot"].at[my_rows, :], lsem.at[4]),
    ]
    loads += [
        pltpu.make_async_copy(cos_h, b["cos"], lsem.at[0]),
        pltpu.make_async_copy(sin_h, b["sin"], lsem.at[1]),
    ]
    strips = [[pltpu.make_async_copy(ref.at[:, k, :], b["pm"[i]].at[k], psem.at[i, k]) for k in range(BLOCKS)]
              for i, ref in enumerate((p_h, m_h))]
    order = [kd + c for c in range(CH) for kd in (0, 4, 8, 12)]
    for k in order:
        strips[0][k].start()
    for load in loads:
        load.start()
    for k in order:
        strips[1][k].start()

    barrier = pltpu.get_barrier_semaphore()
    partners = [dev(cc=other), dev(zz=1 - zh), dev(zz=1 - zh, cc=other)]
    partners += [side[a][d] for a in ("x", "y") for d in ("r", "l")]
    partners += [dev(xx=up(x, 2)), dev(yy=up(y, 2))]
    partners += [dev(r=up(rep, d), cc=cc) for d in sorted({distance, 4 - distance}) for cc in (core, other)]
    for partner in partners:
        pl.semaphore_signal(barrier, inc=1, device_id=partner, device_id_type=MESH)

    def make_pieces(c):
        for kd in (0, 4, 8, 12):
            strips[0][kd + c].wait()
        for d in range(2):
            v = [b["p"][d * 4 + c], b["p"][8 + d * 4 + c], jnp.zeros((8, 128), F32)]
            b["piece"][c, d] = jnp.concatenate(v, axis=0).astype(BF16)

    quad = [(dev(cc=other), zh * 2 + other, other),
            (dev(zz=1 - zh), (1 - zh) * 2 + core, core),
            (dev(zz=1 - zh, cc=other), (1 - zh) * 2 + other, other)]
    my_slot = zh * 2 + core

    def quad_send(c):
        for k, (where, _, d) in enumerate(quad):
            rc(b["piece"].at[c, d], b["pin"].at[c, my_slot], c, M_QUAD + k, where).start()

    def quad_done(c):
        for k, (where, slot, d) in enumerate(quad):
            rc(b["piece"].at[c, d], b["pin"].at[c, slot], c, M_QUAD + k, where).wait_recv()
        b["pin"][c, my_slot] = b["piece"][c, core]
        v = [b["pin"][c, s].astype(F32) for s in range(4)]
        for kv in range(2):
            block = jnp.concatenate([u[kv * OWN:(kv + 1) * OWN] for u in v], axis=0)
            b["w"][c, y, pl.ds(m16(x * ROWS), ROWS), pl.ds(kv * 128, 128)] = block.astype(BF16)

    def w_unit(c, half, phase, j, part):
        lanes = pl.ds(half * 128, 128)
        w = b["w"]
        if phase == 0:
            at, n = dict(all=(0, ROWS), p=(0, 80), q=(80, 64))[part]
            if half == 0:
                return w.at[c, y, pl.ds(m16(j * ROWS + at), n), lanes]
            return w.at[c, j, pl.ds(m16(x * ROWS + at), n), lanes]
        if half == 0:
            at, n = dict(all=(0, 576), p=(0, 288), q=(288, 288))[part]
            return w.at[c, j, pl.ds(at, n), lanes]
        at, n = dict(all=(0, 4), p=(0, 2), q=(2, 2))[part]
        return w.at[c, pl.ds(at, n), pl.ds(m16(j * ROWS), ROWS), lanes]

    def far(half, phase):
        return dev(xx=up(x, 2)) if half == phase else dev(yy=up(y, 2))

    def ag_copy(c, half, phase, k, j):
        s = axis_of(half, phase)
        unit = w_unit(c, half, phase, j, ("all", "all", "p", "q")[k])
        return rc(unit, unit, c, M_AG + half * 8 + phase * 4 + k, s["r"] if k % 2 == 0 else s["l"])

    def ag_start(c, half, phase):
        me = axis_of(half, phase)["me"]
        ag_copy(c, half, phase, 0, me).start()
        ag_copy(c, half, phase, 1, me).start()

    def ag_mid(c, half, phase):
        me = axis_of(half, phase)["me"]
        ag_copy(c, half, phase, 0, up(me, 3)).wait_recv()
        ag_copy(c, half, phase, 2, up(me, 3)).start()
        ag_copy(c, half, phase, 1, up(me)).wait_recv()
        ag_copy(c, half, phase, 3, up(me)).start()

    def ag_end(c, half, phase):
        me = axis_of(half, phase)["me"]
        ag_copy(c, half, phase, 2, up(me, 2)).wait_recv()
        ag_copy(c, half, phase, 3, up(me, 2)).wait_recv()

    def transpose_rows(s):
        rows = pl.ds(m16(s * 256, 256), 256)

        def one(k, _):
            cols = pl.ds(m16(k * 256, 256), 256)
            b["tok_t"][cols, rows] = b["tok"][rows, cols].T
            return 0

        lax.fori_loop(0, D // 256, one, 0)

    half_len = LENGTH // 2
    triangle = lax.broadcasted_iota(jnp.int32, (half_len, LENGTH), 0) <= lax.rem(
        lax.broadcasted_iota(jnp.int32, (half_len, LENGTH), 1), half_len)
    scale_in = D ** (-0.5)

    def nt(a, bb):
        return lax.dot_general(a, bb, (((1,), (1,)), ((), ())), preferred_element_type=F32)

    def project(c):
        w = b["w"][c].reshape(D, 256)
        b["joined"][...] = (jnp.dot(b["tok"][...], w, preferred_element_type=F32) * scale_in).astype(BF16)

    def attend(c, s):
        rows = pl.ds(m16(s * 256, 256), 256)
        joined = b["joined"][rows, :]
        key = joined[:, :HEAD].astype(F32)
        val = joined[:, HEAD:]
        cos, sin = b["cos"][...], b["sin"][...]
        rot = (key * cos + pltpu.roll(key, 64, 1) * sin).astype(BF16)
        d_val, d_rot = [], []
        for block in range(2):
            at = pl.ds(m16(s * LENGTH + block * half_len, half_len), half_len)
            cols = [pl.ds(m16(c * 256 + head * 128, 128), 128) for head in range(2)]
            qh = jnp.concatenate([b["q"][at, col] for col in cols], axis=0)
            ch = jnp.concatenate([b["cot"][at, col] for col in cols], axis=0)
            keys = half_len * (block + 1)
            bent = jnp.tanh(nt(rot[:keys], qh) * (SCORE_SCALE / SOFT_CAP))
            weights = jnp.exp2(bent * (SOFT_CAP * LOG2E))
            masked = jnp.where(triangle, weights[keys - half_len:], 0.0)
            weights = masked if block == 0 else jnp.concatenate([weights[:half_len], masked], axis=0)
            shares = weights * (1.0 / jnp.sum(weights, axis=0, keepdims=True))
            d_val.append(jnp.dot(shares.astype(BF16), ch, preferred_element_type=F32))
            share_grad = nt(val[:keys], ch)
            mean = jnp.sum(shares * share_grad, axis=0, keepdims=True)
            score = shares * (share_grad - mean) * (SCORE_SCALE - bent * bent * SCORE_SCALE)
            d_rot.append(jnp.dot(score.astype(BF16), qh, preferred_element_type=F32))
        d_val, d_rot = (jnp.concatenate([hi[:half_len] + lo, hi[half_len:]], axis=0) for lo, hi in (d_val, d_rot))
        d_key = d_rot * cos - pltpu.roll(d_rot, 64, 1) * sin
        b["grads"][rows, :] = (jnp.concatenate([d_key, d_val], axis=1) * scale_in).astype(BF16)

    def gradient(c, part):
        rows = pl.ds(m16(part * 1152, 128), 1152)
        v = jnp.dot(b["tok_t"][rows, :], b["grads"][...], preferred_element_type=F32).reshape(2, 576, 256)
        at = pl.ds(part * 2, 2)
        b["f"][c, at] = v
        b["g"][c, at] = v.astype(BF16)

    def unit(name, c, half, phase, j, part):
        if phase == 0:
            ref = b["f" if name == "f" else "g"]
            if half == 0:
                return ref.at[c, pl.ds(0 if part == "p" else 2, 2), pl.ds(m16(j * ROWS), ROWS), pl.ds(0, 128)]
            return ref.at[c, j, pl.ds(0 if part == "p" else 288, 288), pl.ds(128, 128)]
        ref = b["h" if name == "f" else "hb"]
        return ref.at[c, half, j, pl.ds(0, 80) if part == "p" else pl.ds(80, 64), :]

    def buf(c, half, phase, name):
        return b["xy"[phase] + str(half) + name].at[c]

    RS_DST = ("al", "ar", "bl", "br", "cl", "cr")
    RS_PART = ("p", "q", "q", "p", "p", "q")

    def rs_copy(c, half, phase, k):
        s = axis_rs(half, phase)
        me = s["me"]
        if k < 4:
            j = (up(me, 2), up(me, 2), up(me), up(me, 3))[k]
            src = unit("g", c, half, phase, j, RS_PART[k])
        else:
            src = buf(c, half, phase, "tr" if k == 4 else "tl")
        return rc(src, buf(c, half, phase, RS_DST[k]), c, M_RS + half * 12 + phase * 6 + k,
                  s["r"] if k % 2 == 0 else s["l"])

    def rs_start(c, half, phase):
        for k in range(4):
            rs_copy(c, half, phase, k).start()

    def rs_mid(c, half, phase):
        me = axis_rs(half, phase)["me"]
        for k, j, part, arrived, out in ((0, up(me), "p", "al", "tr"), (1, up(me, 3), "q", "ar", "tl")):
            rs_copy(c, half, phase, k).wait_recv()
            total = unit("f", c, half, phase, j, part)[...] + buf(c, half, phase, arrived)[...].astype(F32)
            buf(c, half, phase, out)[...] = total.astype(BF16)
            rs_copy(c, half, phase, 4 + k).start()

    def rs_end(c, half, phase):
        me = axis_rs(half, phase)["me"]
        for k in range(2, 6):
            rs_copy(c, half, phase, k).wait_recv()
        for part, one, two in (("p", "cl", "br"), ("q", "bl", "cr")):
            total = (unit("f", c, half, phase, me, part)[...]
                     + buf(c, half, phase, one)[...].astype(F32) + buf(c, half, phase, two)[...].astype(F32))
            if phase == 0:
                at = pl.ds(0 if part == "p" else 2, 2)
                total = total.reshape(2, ROWS, 128)
                b["h"][c, half, at] = total
                b["hb"][c, half, at] = total.astype(BF16)
            else:
                at = pl.ds(0, 80) if part == "p" else pl.ds(80, 64)
                b["e"][c, at, pl.ds(half * 128, 128)] = total

    def z_copy(c):
        return rc(b["zs"].at[c], b["zr"].at[c], c, M_Z, dev(zz=1 - zh))

    def z_send(c):
        v = b["e"][c]
        b["zs"][c] = jnp.where(zh == 0, v[64:], v[:80]).astype(BF16)
        z_copy(c).start()

    def fix_copy(c, slot):
        return rc(b["fs"].at[c], b["gx"].at[c, slot], c, M_FIX, dev(cc=other))

    def gossip_copy(c, rel, slot):
        to = core if rel == 0 else other
        return rc(b["gb"].at[c, to], b["gp"].at[c, slot], c, M_GOS + rel,
                  dev(r=up(rep, distance), cc=to))

    def z_done(c):
        z_copy(c).wait_recv()
        v = b["e"][c]
        r = b["zr"][c].astype(F32)
        total = jnp.where(zh == 0, v[:72], v[72:]) + jnp.where(zh == 0, r[:72], r[8:])
        first, last = (jnp.concatenate([total[r:r + OWN, :128], total[r:r + OWN, 128:]], axis=0) for r in (0, OWN))
        pad = jnp.zeros((8, 128), F32)
        b["gb"][c, 0] = jnp.concatenate([first, pad], axis=0).astype(BF16)
        b["gb"][c, 1] = jnp.concatenate([last, pad], axis=0).astype(BF16)
        for rel in (0, 1):
            gossip_copy(c, rel, core).start()
        b["fs"][c] = jnp.where(core == 0, last, first)
        fix_copy(c, core).start()
        b["gx"][c, core] = jnp.where(core == 0, first, last)

    t = step_ref[0]
    learn_now = LEARN_RATE * (t.astype(F32) + 1.0) / WARM_SPAN

    def out_copy(i, k):
        return pltpu.make_async_copy(b[("out_p", "out_m")[i]].at[k], (outp_h, outm_h)[i].at[:, k, :], osem.at[i, k])

    def finish(c):
        fix_copy(c, other).wait_recv()
        for rel in (0, 1):
            gossip_copy(c, rel, core if rel == 0 else other).wait_recv()
        for d in range(2):
            own = b["gx"][c, d]
            peer = b["gp"][c, d].astype(F32)
            for kv in range(2):
                at = kv * 8 + d * 4 + c
                mom = MOMENTUM_DECAY * b["m"][at] + own[kv * OWN:(kv + 1) * OWN]
                mom2 = MOMENTUM_DECAY * b["peer"][1, at] + peer[kv * OWN:(kv + 1) * OWN]
                b["out_m"][at] = mom + mom2
                b["out_p"][at] = (b["p"][at] - learn_now * mom) + (b["peer"][0, at] - learn_now * mom2)
                for i in range(2):
                    out_copy(i, at).start()

    def exchange(k, slot):
        src = (tok_h.at[0], q_h.at[0, :, other_cols], cot_h.at[0, :, other_cols])[k]
        dst = b[("tok", "q", "cot")[k]].at[pl.ds(m16(slot * TOK, TOK), TOK), :]
        return pltpu.make_async_remote_copy(
            src_ref=src, dst_ref=dst, send_sem=gssem.at[k], recv_sem=grsem.at[k],
            device_id=dev(cc=other), device_id_type=MESH)

    def peer_copy(k):
        at = 3 + k
        return pltpu.make_async_remote_copy(
            src_ref=b["pm"[k]], dst_ref=b["peer"].at[k], send_sem=gssem.at[at],
            recv_sem=grsem.at[at], device_id=dev(r=up(rep, distance)), device_id_type=MESH)

    def each(*steps):
        def body(c, _):
            for step in steps:
                step(c)
            return 0

        lax.fori_loop(0, CH, body, 0)

    def halves(step, phase):
        def run(c):
            step(c, 0, phase)
            step(c, 1, phase)

        return run

    def agd_copy(c, half, phase, k, j):
        s = axis_of(half, phase)
        block = w_unit(c, half, phase, j, "all")
        return rc(block, block, c, M_AG + half * 8 + phase * 4 + k, (s["r"], s["l"], far(half, phase))[k])

    def agd_start(c, half, phase):
        me = axis_of(half, phase)["me"]
        for k in (2, 0, 1):
            agd_copy(c, half, phase, k, me).start()

    def agd_end(c, half, phase):
        me = axis_of(half, phase)["me"]
        for k, by in ((0, 3), (1, 1), (2, 2)):
            agd_copy(c, half, phase, k, up(me, by)).wait_recv()

    def rsd_copy(c, half, phase, k, part):
        s = axis_rs(half, phase)
        me = s["me"]
        j = (up(me), up(me, 3), up(me, 2))[k]
        src = unit("g", c, half, phase, j, part)
        name = {"p": ("al", "br", "cl"), "q": ("ar", "bl", "cr")}[part][k]
        return rc(src, buf(c, half, phase, name), c, M_RS + half * 12 + phase * 6 + k * 2 + (part == "q"),
                  (s["r"], s["l"], far(half, phase))[k])

    def rsd_start(c, half, phase):
        for k in (2, 0, 1):
            for part in ("p", "q"):
                rsd_copy(c, half, phase, k, part).start()

    def rsd_end(c, half, phase):
        me = axis_rs(half, phase)["me"]
        for part in ("p", "q"):
            for k in range(3):
                rsd_copy(c, half, phase, k, part).wait_recv()
        for part, names in (("p", ("al", "br", "cl")), ("q", ("ar", "bl", "cr"))):
            total = unit("f", c, half, phase, me, part)[...]
            for name in names:
                total += buf(c, half, phase, name)[...].astype(F32)
            if phase == 0:
                at = pl.ds(0 if part == "p" else 2, 2)
                total = total.reshape(2, ROWS, 128)
                b["h"][c, half, at] = total
                b["hb"][c, half, at] = total.astype(BF16)
            else:
                at = pl.ds(0, 80) if part == "p" else pl.ds(80, 64)
                b["e"][c, at, pl.ds(half * 128, 128)] = total

    agd0s, agd0e = (halves(step, 0) for step in (agd_start, agd_end))
    ag1s, ag1m, ag1e = (halves(step, 1) for step in (ag_start, ag_mid, ag_end))
    rs0s, rs0m, rs0e = (halves(step, 0) for step in (rs_start, rs_mid, rs_end))
    rsd1s, rsd1e = (halves(step, 1) for step in (rsd_start, rsd_end))

    def when(condition, *steps):
        def run():
            for step, c in steps:
                step(c)

        pl.when(condition)(run)

    make_pieces(0)
    pl.semaphore_wait(barrier, len(partners))
    quad_send(0)
    for c in range(1, CH):
        make_pieces(c)
        quad_send(c)
    exchange(0, core).start()
    loads[0].wait()
    quad_done(0)
    agd0s(0)
    transpose_rows(core * 2)
    for k in (1, 2):
        exchange(k, core).start()
    quad_done(1)
    agd0s(1)
    agd0e(0)
    ag1s(0)
    quad_done(2)
    agd0s(2)
    transpose_rows(core * 2 + 1)
    agd0e(1)
    ag1s(1)
    quad_done(3)
    agd0s(3)
    ag1m(0)
    for k in range(BLOCKS):
        strips[1][k].wait()
    for k in range(2):
        peer_copy(k).start()
    exchange(0, other).wait_recv()
    transpose_rows(other * 2)
    agd0e(2)
    ag1s(2)
    ag1m(1)
    agd0e(3)
    ag1s(3)
    transpose_rows(other * 2 + 1)
    for k in (1, 2):
        exchange(k, other).wait_recv()
    for k in (1, 2, 3, 4):
        loads[k].wait()

    def work(c):
        ag1e(c)

        project(c)
        when(c == 1, (ag1m, 3))
        when(c > 1, (rs0e, c - 2), (rsd1s, c - 2))

        def pair(i, _):
            attend(c, 2 * i)
            attend(c, 2 * i + 1)
            when((c == 0) & (i == 0), (ag1m, 2))
            when((c == CH - 1) & (i == 0), (z_done, 0))
            when((c > 0) & (i == 1), (rs0m, c - 1))
            return 0

        def part(i, _):
            gradient(c, i)
            when((c > 1) & (i == 0), (rsd1e, c - 2), (z_send, c - 2))
            return 0

        lax.fori_loop(0, 2, pair, 0)
        lax.fori_loop(0, 2, part, 0)
        rs0s(c)

    def drain_gather(c):
        for k, (where, _, d) in enumerate(quad):
            rc(b["piece"].at[c, d], b["pin"].at[c, my_slot], c, M_QUAD + k, where).wait_send()
        for half in range(2):
            me = axis_of(half, 0)["me"]
            for k in range(3):
                agd_copy(c, half, 0, k, me).wait_send()
            me = axis_of(half, 1)["me"]
            for k in range(4):
                ag_copy(c, half, 1, k, up(me, (0, 0, 3, 1)[k])).wait_send()

    def drain_wide(c):
        for half in range(2):
            for k in range(6):
                rs_copy(c, half, 0, k).wait_send()

    def drain_narrow(c):
        for half in range(2):
            for k in range(3):
                for part in ("p", "q"):
                    rsd_copy(c, half, 1, k, part).wait_send()

    def drain_end(c):
        z_copy(c).wait_send()
        fix_copy(c, core).wait_send()
        for rel in (0, 1):
            gossip_copy(c, rel, core).wait_send()
        for i in range(2):
            for k in (0, 4, 8, 12):
                out_copy(i, k + c).wait()

    each(work)
    last = CH - 1
    rs0e(last - 1)
    rsd1s(last - 1)
    rs0m(last)
    z_done(last - 2)
    rsd1e(last - 1)
    z_send(last - 1)
    rs0e(last)
    rsd1s(last)
    for k in range(2):
        peer_copy(k).wait_recv()
    finish(0)
    z_done(last - 1)
    rsd1e(last)
    z_send(last)
    finish(1)
    each(drain_gather)
    each(drain_wide)
    drain_narrow(0)
    drain_narrow(1)
    finish(last - 1)
    drain_narrow(2)
    for k in range(3):
        exchange(k, core).wait_send()
    for k in range(2):
        peer_copy(k).wait_send()
    z_done(last)
    drain_narrow(3)
    for c in range(last):
        drain_end(c)
    finish(last)
    drain_end(last)


def step_kernel(distance):
    anywhere = pl.BlockSpec(memory_space=pl.ANY)
    return pl.pallas_call(
        functools.partial(kernel, distance),
        out_shape=[jax.ShapeDtypeStruct((OWN, BLOCKS, 128), F32)] * 2,
        in_specs=[pl.BlockSpec(memory_space=pltpu.SMEM)] + [anywhere] * 7,
        out_specs=[anywhere, anywhere],
        scratch_shapes=[pltpu.VMEM(shape, dtype) for shape, dtype in SCRATCH.values()]
        + [
            pltpu.SemaphoreType.DMA((CH, M_ALL)),
            pltpu.SemaphoreType.DMA((CH, M_ALL)),
            pltpu.SemaphoreType.DMA((5,)),
            pltpu.SemaphoreType.DMA((5,)),
            pltpu.SemaphoreType.DMA((5,)),
            pltpu.SemaphoreType.DMA((2, BLOCKS)),
            pltpu.SemaphoreType.DMA((2, BLOCKS)),
        ],
        compiler_params=pltpu.CompilerParams(
            collective_id=distance, has_side_effects=True, vmem_limit_bytes=60 * 2**20),
        cost_estimate=pl.CostEstimate(flops=13 * 10**9, bytes_accessed=10**7, transcendentals=4 * 10**6),
    )


def shards(step_index, tokens, queries, cotangent, params, momentum):
    cos, sin = rope_tables()
    operands = (step_index, tokens, queries, cotangent, params.reshape(OWN, BLOCKS, 128),
                momentum.reshape(OWN, BLOCKS, 128), jnp.asarray(cos), jnp.asarray(sin))
    sum_p, sum_m = lax.cond(
        (step_index[0] & 1) == 0, *[lambda *xs, d=d: tuple(step_kernel(d)(*xs)) for d in (1, 2)], *operands)
    return (0.5 * sum_p).reshape(1, OWN, WIDE), (0.5 * sum_m).reshape(1, OWN, WIDE)


def solution(mesh):
    rows = P("rep", "fsdp", None)
    return jax.shard_map(
        shards,
        mesh=mesh,
        in_specs=(P(), rows, rows, rows, rows, rows),
        out_specs=(rows, rows),
        check_vma=False,
    )
```
